32 devices in a mesh: section: 4 (over y, x), tile: 8 (over z, core).
Axes of the slice: x: 2, y: 2, z: 4, core: 2. Of those that a mesh axis runs over, the one named last changes fastest.
Arguments:
- cams: bfloat16 [4, 4096, 768], P(None, 'tile'), may hold values from -6 to 6
- vit_up: bfloat16 [4, 768, 1536], P('section'), may hold values from -0.21875 to 0.21875
- vit_down: bfloat16 [4, 1536, 768], P('section'), may hold values from -0.15625 to 0.15625
- proj: bfloat16 [768, 256], replicated, may hold values from -0.21875 to 0.21875
- frustum_tiles: bfloat16 [8, 8, 128, 128], P('tile'), may hold values from -0.4375 to 0.4375
- src_block: int32 [8, 8], P('tile'), may hold values from 0 to 3
- dst_block: int32 [8, 8], P('tile'), may hold values from 0 to 4
- live: int32 [8, 8], P('tile'), may hold values 0 or 1
- render_up: bfloat16 [256, 512], replicated, may hold values from -0.375 to 0.375
- render_down: bfloat16 [512, 256], replicated, may hold values from -0.25 to 0.25
- decode_up: bfloat16 [256, 512], replicated, may hold values from -0.375 to 0.375
- decode_down: bfloat16 [512, 256], replicated, may hold values from -0.25 to 0.25
- pred_grad: bfloat16 [4, 5120, 256], P('section', 'tile'), may hold values from -6 to 6
Outputs:
- prediction: bfloat16 [4, 5120, 256], P('section', 'tile')
- grad_proj: float32 [768, 256], replicated
- grad_render_up: float32 [256, 512], replicated
- grad_render_down: float32 [512, 256], replicated
- grad_decode_up: float32 [256, 512], replicated
- grad_decode_down: float32 [512, 256], replicated
The draws below stay inside these ranges and needn't reach their ends.
All inputs are finite; a program needn't handle non-finite values. No bound on the sum of `live` on one device may be relied on, other than what follows from the above.
Results may differ from the reference program's by a relative error of at most 0.025.
Values may be sent and summed in bfloat16 or wider, within the bound.
No kernel may reach another device: no remote copies, remote signals or barrier semaphores. Data moves between devices by JAX's collectives and lax.ppermute only.
A program may use at most 128 MiB of HBM per device.

```python
import math
import jax
import jax.numpy as jnp
from jax import lax

D = 768
FFV = 1536
C = 256
FFB = 512
BLK = 128
CAM_BLK = 4
BEV_BLK = 5
LAYERS = 4
MICRO = 4
TOKENS = 4096
CELLS = 5120
N_TILE = 8


def place_ends(entries, key, least, largest):
    spot = [jax.random.randint(jax.random.fold_in(key, axis), (), 0, length) for axis, length in enumerate(entries.shape)]
    widest = entries.shape.index(max(entries.shape))
    next_to = spot[:widest] + [(spot[widest] + 1) % entries.shape[widest]] + spot[widest + 1:]
    return entries.at[tuple(spot)].set(least).at[tuple(next_to)].set(largest)


def shard_levels(stream_key, extent, shards, least, high):
    level = 1.0
    for position, parts in shards:
        steps = jax.random.uniform(jax.random.fold_in(jax.random.fold_in(stream_key, 6), position), (parts,), jnp.float32, least / len(shards), high / len(shards))
        level = level * jnp.repeat(jnp.exp(steps), extent[position] // parts).reshape((-1,) + (1,) * (len(extent) - 1 - position))
    return level


def scatter_about(stream_key, dims, scale, most, shards=(), held_as=jnp.bfloat16):
    values = scale * jax.random.normal(stream_key, dims, jnp.float32)
    if shards:
        values = values * shard_levels(stream_key, dims, shards, -0.22, 0.18)
    return jnp.clip(values, -most, most).astype(held_as)


def setup_inputs(seed: int = 0) -> dict:
    key_of = jax.random.split(jax.random.key(seed), 14)
    cams = scatter_about(key_of[0], (MICRO, TOKENS, D), 1.0, 6.0, ((1, 8),))
    vit_up = scatter_about(key_of[1], (LAYERS, D, FFV), D ** -0.5, 0.21875, ((0, 4),))
    vit_down = scatter_about(key_of[2], (LAYERS, FFV, D), FFV ** -0.5, 0.15625, ((0, 4),))
    proj = scatter_about(key_of[3], (D, C), D ** -0.5, 0.21875)
    frustum_tiles = scatter_about(key_of[4], (N_TILE, N_TILE, BLK, BLK), (BLK * N_TILE // BEV_BLK) ** -0.5, 0.4375, ((0, 8),))
    src_block = place_ends(jax.random.randint(key_of[5], (N_TILE, N_TILE), 0, CAM_BLK), jax.random.fold_in(key_of[5], 1), 0, CAM_BLK - 1).astype(jnp.int32)
    dst_block = place_ends(jax.random.randint(key_of[6], (N_TILE, N_TILE), 0, BEV_BLK), jax.random.fold_in(key_of[6], 1), 0, BEV_BLK - 1).astype(jnp.int32)
    live = place_ends((jax.random.randint(key_of[7], (N_TILE, N_TILE), 0, 4) < 3).astype(jnp.int32), jax.random.fold_in(key_of[7], 1), 0, 1)
    render_up = scatter_about(key_of[8], (C, FFB), C ** -0.5, 0.375)
    render_down = scatter_about(key_of[9], (FFB, C), FFB ** -0.5, 0.25)
    decode_up = scatter_about(key_of[10], (C, FFB), C ** -0.5, 0.375)
    decode_down = scatter_about(key_of[11], (FFB, C), FFB ** -0.5, 0.25)
    pred_grad = scatter_about(key_of[12], (MICRO, CELLS, C), 1.0, 6.0, ((0, 4), (1, 8)))
    return {"cams": cams, "vit_up": vit_up, "vit_down": vit_down, "proj": proj, "frustum_tiles": frustum_tiles, "src_block": src_block, "dst_block": dst_block, "live": live, "render_up": render_up, "render_down": render_down, "decode_up": decode_up, "decode_down": decode_down, "pred_grad": pred_grad}


eps = 1e-05

def encoder_layer(state, w_up, w_down):
    widened = state.astype(jnp.float32)
    scaling = lax.rsqrt(lax.optimization_barrier(jnp.mean(widened * widened, axis=-1, keepdims=True)) + eps)
    normed = (widened * scaling).astype(jnp.bfloat16)
    hidden = jax.nn.gelu(jnp.dot(normed, w_up, preferred_element_type=jnp.float32)).astype(jnp.bfloat16)
    return (widened + jnp.dot(hidden, w_down, preferred_element_type=jnp.float32)).astype(jnp.bfloat16)

def contract_rows(left, right):
    return lax.dot_general(left, right, (((0,), (0,)), ((), ())), preferred_element_type=jnp.float32)

def against_rows(left, right):
    return lax.dot_general(left, right, (((1,), (1,)), ((), ())), preferred_element_type=jnp.float32)

def heads_forward(bev_grid, weights):
    state = bev_grid
    stored = []
    for w_up, w_down in weights:
        scaling = lax.rsqrt(lax.optimization_barrier(jnp.mean(state * state, axis=-1, keepdims=True)) + eps)
        normed = (state * scaling).astype(jnp.bfloat16)
        preact = jnp.dot(normed, w_up, preferred_element_type=jnp.float32)
        hidden = jax.nn.gelu(preact).astype(jnp.bfloat16)
        stored.append((state, scaling, normed, preact, hidden))
        state = state + jnp.dot(hidden, w_down, preferred_element_type=jnp.float32)
    return (state.astype(jnp.bfloat16), stored)

def heads_backward(cotangent, stored, weights):
    grad_state = cotangent
    gradients = []
    for saved_block, pair in zip(stored[::-1], weights[::-1]):
        state, scaling, normed, preact, hidden = saved_block
        w_up, w_down = pair
        rounded = grad_state.astype(jnp.bfloat16)
        grad_down = contract_rows(hidden, rounded)
        grad_hidden = against_rows(rounded, w_down)
        gelu_slope = jax.jvp(jax.nn.gelu, (preact,), (jnp.ones_like(preact),))[1]
        grad_pre = (grad_hidden * gelu_slope).astype(jnp.bfloat16)
        grad_up = contract_rows(normed, grad_pre)
        grad_normed = against_rows(grad_pre, w_up)
        unit_rows = state * scaling
        grad_state = grad_state + scaling * (grad_normed - unit_rows * lax.optimization_barrier(jnp.mean(grad_normed * unit_rows, axis=-1, keepdims=True)))
        gradients = [grad_up, grad_down] + gradients
    return (grad_state, gradients)

def reference(cams, vit_up, vit_down, proj, frustum_tiles, src_block, dst_block, live, render_up, render_down, decode_up, decode_down, pred_grad):
    weights = ((render_up, render_down), (decode_up, decode_down))
    scale_factor = 1.0 / math.sqrt(MICRO * CELLS)
    cam_range = jnp.arange(CAM_BLK, dtype=jnp.int32)
    bev_range = jnp.arange(BEV_BLK, dtype=jnp.int32)
    slot_range = jnp.arange(N_TILE, dtype=jnp.int32)
    alive_flags = live.astype(jnp.float32)

    def one_batch(inputs):
        tokens, grad_out = inputs
        encoded = tokens
        for layer_number in range(LAYERS):
            encoded = encoder_layer(encoded, vit_up[layer_number], vit_down[layer_number])
        projected = jnp.dot(encoded, proj, preferred_element_type=jnp.float32).astype(jnp.bfloat16)
        blocks = projected.reshape(N_TILE, CAM_BLK, BLK, C)

        def join_sender(running, sender):
            own_blocks, slot_tiles, sources, targets, alive_row = sender
            chosen = jnp.take(own_blocks, sources, axis=0).astype(jnp.float32)
            pieces = (jnp.einsum('pij,pjc->pic', slot_tiles.astype(jnp.float32), chosen) * alive_row[:, None, None]).astype(jnp.bfloat16)
            target_pick = (targets[:, None] == bev_range[None, :]).astype(jnp.float32)
            return (running + target_pick[:, :, None, None] * pieces.astype(jnp.float32)[:, None], None)
        initial = jnp.zeros((N_TILE, BEV_BLK, BLK, C), jnp.float32)
        bev_blocks, unused = lax.scan(join_sender, initial, (blocks, frustum_tiles, src_block, dst_block, alive_flags))
        prediction, stored = heads_forward(bev_blocks.reshape(CELLS, C), weights)
        cotangent = grad_out.astype(jnp.float32) * scale_factor
        grad_grid, gradients = heads_backward(cotangent, stored, weights)
        grad_blocks = grad_grid.reshape(N_TILE, BEV_BLK, BLK, C)

        def split_sender(carried, sender):
            slot_tiles, sources, targets, alive_row = sender
            grad_pieces = grad_blocks[slot_range, targets].astype(jnp.bfloat16)
            grad_pieces = lax.optimization_barrier(grad_pieces).astype(jnp.float32)
            grad_chosen = jnp.einsum('pij,pic->pjc', slot_tiles.astype(jnp.float32), grad_pieces) * alive_row[:, None, None]
            source_pick = (sources[:, None] == cam_range[None, :]).astype(jnp.float32)
            return (carried, jnp.einsum('pk,pjc->kjc', source_pick, grad_chosen, precision=lax.Precision.HIGHEST))
        unused_carry, grad_rows = lax.scan(split_sender, jnp.zeros((), jnp.float32), (frustum_tiles, src_block, dst_block, alive_flags))
        grad_rows = grad_rows.reshape(TOKENS, C).astype(jnp.bfloat16)
        grad_proj = contract_rows(encoded, grad_rows)
        return (prediction, grad_proj, gradients[0], gradients[1], gradients[2], gradients[3])
    results = lax.map(one_batch, (cams, pred_grad))
    return (results[0], lax.optimization_barrier(jnp.sum(results[1], axis=0)), lax.optimization_barrier(jnp.sum(results[2], axis=0)), lax.optimization_barrier(jnp.sum(results[3], axis=0)), lax.optimization_barrier(jnp.sum(results[4], axis=0)), lax.optimization_barrier(jnp.sum(results[5], axis=0)))
```

```python
import functools
import math

import jax
import jax.numpy as jnp
from jax import lax
from jax.experimental import pallas as pl
from jax.experimental.pallas import tpu as pltpu
from jax.sharding import PartitionSpec as P

eps = 1e-05
gelu_inner = math.sqrt(2.0 / math.pi)
gelu_cubic = 0.044715
vmem_bytes = 50 * 1024 * 1024


def gelu(value):
    inner = gelu_inner * (value + gelu_cubic * (value * value * value))
    half = 0.5 * value
    return half + half * jnp.tanh(inner)


def gelu_and_slope(value):
    square = value * value
    reach = jnp.tanh(gelu_inner * value * (1.0 + gelu_cubic * square))
    half = 0.5 * value
    up_to_one = 0.5 + 0.5 * reach
    slope = up_to_one + half * (1.0 - reach * reach) * (
        gelu_inner + (3.0 * gelu_inner * gelu_cubic) * square
    )
    return (value * up_to_one, slope)


def plain(left, right):
    return jnp.dot(left, right, preferred_element_type=jnp.float32)


def contract_rows(left, right):
    return lax.dot_general(
        left, right, (((0,), (0,)), ((), ())), preferred_element_type=jnp.float32
    )


def against_rows(left, right):
    return lax.dot_general(
        left, right, (((1,), (1,)), ((), ())), preferred_element_type=jnp.float32
    )


def encode_kernel(
    names,
    block_rows,
    place_ref,
    sources_ref,
    alive_ref,
    slot_of_ref,
    cams_ref,
    own_up_ref,
    own_down_ref,
    proj_ref,
    tiles_ref,
    *rest,
):
    parts = dict(zip(names, rest[: len(names)]))
    encoded_ref, pieces_ref = rest[len(names) : len(names) + 2]
    state, ups, downs, projected, state_sem, up_sems, down_sems = rest[len(names) + 2 :]
    section, core, zone = place_ref[0], place_ref[1], place_ref[2]
    layers, halves, half = ups.shape[:3]
    window = parts["x_up_window"].shape[0]
    missing = half - window

    load_state = pltpu.make_async_copy(cams_ref.at[section], state, state_sem)
    load_state.start()

    def pieces_of(relation, kind):
        found = []
        for side in ("", "other_"):
            at = core if side == "" else 1 - core
            name = f"{side}{relation}_{kind}"
            if name in parts:
                found.append((parts[name], at, 0, half))
            else:
                found.append((parts[name + "_window"], at, zone * missing, window))
                found.append((parts[name + "_missing"], at, (1 - zone) * window, missing))
        return found

    for layer in range(layers):
        for number, relation in enumerate(("own", "x", "y", "d")):

            @pl.when(jnp.bitwise_xor(section, layer) == number)
            def load(layer=layer, relation=relation):
                if relation == "own":
                    for at in range(halves):
                        pltpu.make_async_copy(
                            own_up_ref.at[:, pl.ds(at * half, half)],
                            ups.at[layer, at],
                            up_sems.at[layer],
                        ).start()
                        pltpu.make_async_copy(
                            own_down_ref.at[pl.ds(at * half, half)],
                            downs.at[layer, at],
                            down_sems.at[layer],
                        ).start()
                    return
                for kind, held, sems in (("up", ups, up_sems), ("down", downs, down_sems)):
                    for ref, at, first, count in pieces_of(relation, kind):
                        start = first if isinstance(first, int) else pl.multiple_of(first, 16)
                        pltpu.make_async_copy(
                            ref, held.at[layer, at, pl.ds(start, count)], sems.at[layer]
                        ).start()

    load_state.wait()
    for layer in range(layers):
        widened = state[...].astype(jnp.float32)
        scaling = lax.rsqrt(jnp.mean(widened * widened, axis=-1, keepdims=True) + eps)
        normed = (widened * scaling).astype(jnp.bfloat16)
        pltpu.make_async_copy(ups.at[layer], ups.at[layer], up_sems.at[layer]).wait()
        pltpu.make_async_copy(downs.at[layer], downs.at[layer], down_sems.at[layer]).wait()
        total = widened
        for at in range(halves):
            for first in range(0, half, half // 2):
                columns = pl.ds(first, half // 2)
                hidden = gelu(plain(normed, ups[layer, at, :, columns])).astype(jnp.bfloat16)
                total = total + plain(hidden, downs[layer, at, columns])
        state[...] = total.astype(jnp.bfloat16)
    encoded_ref[...] = state[...]
    projected[...] = plain(state[...], proj_ref[...]).astype(jnp.bfloat16)

    def slot(number, carry):
        first = pl.multiple_of(sources_ref[number] * block_rows, block_rows)
        piece = plain(tiles_ref[number], projected[pl.ds(first, block_rows)])
        piece = piece * alive_ref[number].astype(jnp.float32)
        pieces_ref[slot_of_ref[number]] = piece.astype(jnp.bfloat16)
        return carry

    lax.fori_loop(0, tiles_ref.shape[0], slot, 0, unroll=tiles_ref.shape[0] <= 8)


def encode(place, sources, alive, slot_of, cams, own_up, own_down, proj, tiles, parts):
    names = tuple(parts)
    tokens, width = cams.shape[1:]
    hidden = own_up.shape[1]
    layers = cams.shape[0]
    half = hidden // 2
    slots, block_rows = tiles.shape[:2]
    channels = proj.shape[1]
    smem = pl.BlockSpec(memory_space=pltpu.SMEM)
    vmem = pl.BlockSpec(memory_space=pltpu.VMEM)
    hbm = pl.BlockSpec(memory_space=pl.ANY)
    return pl.pallas_call(
        functools.partial(encode_kernel, names, block_rows),
        out_shape=(
            jax.ShapeDtypeStruct((tokens, width), jnp.bfloat16),
            jax.ShapeDtypeStruct((slots, block_rows, channels), jnp.bfloat16),
        ),
        in_specs=[smem] * 4 + [hbm] * 3 + [vmem] * 2 + [hbm] * len(names),
        out_specs=(vmem, vmem),
        scratch_shapes=[
            pltpu.VMEM((tokens, width), jnp.bfloat16),
            pltpu.VMEM((layers, 2, width, half), jnp.bfloat16),
            pltpu.VMEM((layers, 2, half, width), jnp.bfloat16),
            pltpu.VMEM((tokens, channels), jnp.bfloat16),
            pltpu.SemaphoreType.DMA,
            pltpu.SemaphoreType.DMA((layers,)),
            pltpu.SemaphoreType.DMA((layers,)),
        ],
        compiler_params=pltpu.CompilerParams(vmem_limit_bytes=vmem_bytes),
        name="encode",
    )(place, sources, alive, slot_of, cams, own_up, own_down, proj, tiles, *parts.values())


def heads_kernel(
    counts,
    scale_factor,
    targets_ref,
    render_up_ref,
    render_down_ref,
    decode_up_ref,
    decode_down_ref,
    pred_grad_ref,
    *rest,
):
    arrived = rest[: len(counts)]
    prediction_ref, gradients_ref = rest[len(counts) : len(counts) + 2]
    returns = rest[len(counts) + 2 : 2 * len(counts) + 2]
    (grid,) = rest[2 * len(counts) + 2 :]
    block_rows = arrived[0].shape[1]
    rows = grid.shape[0]

    grid[...] = jnp.zeros_like(grid)
    number = 0
    for ref, count in zip(arrived, counts):

        def add(at, carry, ref=ref, number=number):
            first = pl.multiple_of(targets_ref[number + at] * block_rows, block_rows)
            grid[pl.ds(first, block_rows)] += ref[at].astype(jnp.float32)
            return carry

        lax.fori_loop(0, count, add, 0, unroll=count <= 8)
        number += count

    weights = ((render_up_ref, render_down_ref), (decode_up_ref, decode_down_ref))
    state = grid[...]
    stored = []
    for w_up, w_down in weights:
        scaling = lax.rsqrt(jnp.mean(state * state, axis=-1, keepdims=True) + eps)
        normed = (state * scaling).astype(jnp.bfloat16)
        value, slope = gelu_and_slope(plain(normed, w_up[...]))
        hidden = value.astype(jnp.bfloat16)
        stored.append((state, scaling, normed, slope, hidden))
        state = state + plain(hidden, w_down[...])
    prediction_ref[...] = state.astype(jnp.bfloat16)

    grad_state = pred_grad_ref[...].astype(jnp.float32) * scale_factor
    width = gradients_ref.shape[-1]
    for block in (1, 0):
        state, scaling, normed, slope, hidden = stored[block]
        w_up, w_down = weights[block]
        rounded = grad_state.astype(jnp.bfloat16)
        grad_down = contract_rows(hidden, rounded).astype(jnp.bfloat16)
        grad_pre = (against_rows(rounded, w_down[...]) * slope).astype(jnp.bfloat16)
        grad_up = contract_rows(normed, grad_pre).astype(jnp.bfloat16)
        gradients_ref[4 * block] = grad_up[:, :width]
        gradients_ref[4 * block + 1] = grad_up[:, width:]
        gradients_ref[4 * block + 2] = grad_down[:width]
        gradients_ref[4 * block + 3] = grad_down[width:]
        grad_normed = against_rows(grad_pre, w_up[...])
        unit_rows = state * scaling
        grad_state = grad_state + scaling * (
            grad_normed - unit_rows * jnp.mean(grad_normed * unit_rows, axis=-1, keepdims=True)
        )
    grid[...] = grad_state
    number = 0
    for ref, count in zip(returns, counts):

        def give(at, carry, ref=ref, number=number):
            first = pl.multiple_of(targets_ref[number + at] * block_rows, block_rows)
            ref[at] = grid[pl.ds(first, block_rows)].astype(jnp.bfloat16)
            return carry

        lax.fori_loop(0, count, give, 0, unroll=count <= 8)
        number += count


def heads(targets, weights, pred_grad, arrived, scale_factor):
    rows, channels = pred_grad.shape
    smem = pl.BlockSpec(memory_space=pltpu.SMEM)
    vmem = pl.BlockSpec(memory_space=pltpu.VMEM)
    counts = tuple(part.shape[0] for part in arrived)
    return pl.pallas_call(
        functools.partial(heads_kernel, counts, scale_factor),
        out_shape=(
            jax.ShapeDtypeStruct((rows, channels), jnp.bfloat16),
            jax.ShapeDtypeStruct((8, channels, channels), jnp.bfloat16),
        )
        + tuple(jax.ShapeDtypeStruct(part.shape, jnp.bfloat16) for part in arrived),
        in_specs=[smem] + [vmem] * (5 + len(arrived)),
        out_specs=(vmem,) * (2 + len(arrived)),
        scratch_shapes=[pltpu.VMEM((rows, channels), jnp.float32)],
        compiler_params=pltpu.CompilerParams(vmem_limit_bytes=vmem_bytes),
        name="heads",
    )(targets, *weights, pred_grad, *arrived)


def proj_grad_kernel(
    counts, order_ref, sources_ref, alive_ref, tiles_ref, encoded_ref, *rest
):
    returned = rest[: len(counts)]
    gradient_ref = rest[len(counts)]
    (rows,) = rest[len(counts) + 1 :]
    block_rows = tiles_ref.shape[1]
    rows[...] = jnp.zeros_like(rows)
    number = 0
    for ref, count in zip(returned, counts):

        def add(at, carry, ref=ref, number=number):
            slot = order_ref[number + at]
            first = pl.multiple_of(sources_ref[slot] * block_rows, block_rows)
            product = contract_rows(tiles_ref[slot], ref[at])
            rows[pl.ds(first, block_rows)] += product * alive_ref[slot].astype(jnp.float32)
            return carry

        lax.fori_loop(0, count, add, 0, unroll=count <= 8)
        number += count
    total = contract_rows(encoded_ref[...], rows[...].astype(jnp.bfloat16))
    gradient_ref[...] = total.astype(jnp.bfloat16).reshape(gradient_ref.shape)


def proj_grad(order, sources, alive, tiles, encoded, returned):
    tokens, width = encoded.shape
    channels = returned[0].shape[-1]
    smem = pl.BlockSpec(memory_space=pltpu.SMEM)
    vmem = pl.BlockSpec(memory_space=pltpu.VMEM)
    counts = tuple(part.shape[0] for part in returned)
    return pl.pallas_call(
        functools.partial(proj_grad_kernel, counts),
        out_shape=jax.ShapeDtypeStruct((8, width // 8, channels), jnp.bfloat16),
        in_specs=[smem] * 3 + [vmem] * (2 + len(returned)),
        out_specs=vmem,
        scratch_shapes=[pltpu.VMEM((tokens, channels), jnp.float32)],
        compiler_params=pltpu.CompilerParams(vmem_limit_bytes=vmem_bytes),
        name="proj_grad",
    )(order, sources, alive, tiles, encoded, *returned)


def to_section(array, flip):
    count = lax.axis_size("section")
    return lax.ppermute(array, "section", [(at, at ^ flip) for at in range(count)])


def to_tile(array, flip):
    count = lax.axis_size("tile")
    return lax.ppermute(array, "tile", [(at, at ^ flip) for at in range(count)])


def rows_from(array, first, count):
    return lax.dynamic_slice_in_dim(array, first, count, 0)


def gather_layers(own_up, own_down, core, zone):
    half = own_down.shape[0] // 2
    window = (half * 7 // 12 + 15) // 16 * 16
    missing = half - window
    shared = window - missing
    up = lax.dynamic_slice_in_dim(own_up, core * half, half, 1)
    down = lax.dynamic_slice_in_dim(own_down, core * half, half, 0)

    def swapped(array):
        return to_tile(rows_from(array, zone * shared, missing), 2)

    x_up = to_section(rows_from(up, zone * missing, window), 1)
    y_down = to_section(rows_from(down, zone * missing, window), 2)
    x_up, y_down, up, down = lax.optimization_barrier((x_up, y_down, up, down))
    d_down = to_section(y_down, 1)
    d_up = to_section(x_up, 2)
    parts = {
        "x_up_window": x_up,
        "y_down_window": y_down,
        "x_up_missing": swapped(x_up),
        "y_down_missing": swapped(y_down),
        "x_down": to_section(down, 1),
        "y_up": to_section(up, 2),
        "d_up_window": d_up,
        "d_down_window": d_down,
        "d_up_missing": swapped(d_up),
        "d_down_missing": swapped(d_down),
    }
    parts.update({"other_" + name: to_tile(part, 1) for name, part in parts.items()})
    return parts


def add_up(left, *others):
    total = left.astype(jnp.float32)
    for other in others:
        total = total + other.astype(jnp.float32)
    return total.astype(jnp.bfloat16)


def total_over_devices(array, section, core):
    count = lax.axis_size("section")
    chips = lax.axis_size("tile") // 2
    mine = rows_from(array, core * count, count)
    others = rows_from(array, (1 - core) * count, count)
    mine = add_up(mine, to_tile(others, 1))

    def pick(number):
        return lax.dynamic_index_in_dim(mine, number, 0, keepdims=False)

    share = add_up(
        pick(section), *[to_section(pick(section ^ flip), flip) for flip in (3, 1, 2)]
    )
    if chips == 4:
        share = add_up(share, *[to_tile(share, 2 * flip) for flip in (2, 3, 1)])
    else:
        groups = [[2 * chip + side for chip in range(chips)] for side in (0, 1)]
        share = lax.psum(share, "tile", axis_index_groups=groups)
    gathered = jnp.stack([share] + [to_section(share, flip) for flip in (1, 2, 3)])
    gathered = jnp.take(gathered, section ^ jnp.arange(count, dtype=jnp.int32), axis=0)
    swapped = to_tile(gathered, 1)
    first = jnp.where(core == 0, gathered, swapped)
    second = jnp.where(core == 0, swapped, gathered)
    return jnp.concatenate([first, second])


def on_device(
    cams,
    vit_up,
    vit_down,
    proj,
    frustum_tiles,
    src_block,
    dst_block,
    live,
    render_up,
    render_down,
    decode_up,
    decode_down,
    pred_grad,
):
    section = lax.axis_index("section").astype(jnp.int32)
    tile = lax.axis_index("tile").astype(jnp.int32)
    tile_count = lax.axis_size("tile")
    micro_count = cams.shape[0]
    core = tile % 2
    chip = tile // 2
    zone = chip % 2
    small = tile_count == 8
    slots = jnp.arange(tile_count, dtype=jnp.int32)
    if small:
        slot_of = (slots // 2 ^ chip) + 4 * ((slots ^ core) % 2)
        order = 2 * (slots // 2 ^ chip) + (slots % 2 ^ core)
    else:
        slot_of = slots
        order = slots

    all_targets = lax.all_gather(dst_block, "tile", axis=0, tiled=True)
    targets = jnp.take(jnp.take(all_targets, tile, axis=1), order)

    parts = gather_layers(vit_up[0], vit_down[0], core, zone)
    place = jnp.stack([section, core, zone])
    encoded, pieces = encode(
        place, src_block[0], live[0], slot_of, cams, vit_up[0], vit_down[0], proj,
        frustum_tiles[0], parts,
    )

    if small:
        crossed = to_tile(pieces[4:], 1)
        both = jnp.stack([pieces[:4], crossed], axis=1)
        far = {flip: to_tile(both[flip], 2 * flip) for flip in (2, 3, 1)}
        arrived = [both[0], far[1], far[2], far[3]]
    else:
        arrived = [lax.all_to_all(pieces, "tile", split_axis=0, concat_axis=0, tiled=True)]

    scale_factor = 1.0 / math.sqrt(micro_count * pred_grad.shape[1] * tile_count)
    weights = (render_up, render_down, decode_up, decode_down)
    prediction, gradients, *returns = heads(
        targets, weights, pred_grad[0], arrived, scale_factor
    )

    if small:
        back = {flip: to_tile(returns[flip], 2 * flip) for flip in (2, 3, 1)}
        back[0] = returns[0]
        returned = []
        for flip in range(4):
            returned += [back[flip][:1], to_tile(back[flip][1:], 1)]
    else:
        returned = [
            lax.all_to_all(returns[0], "tile", split_axis=0, concat_axis=0, tiled=True)
        ]
    head_total = total_over_devices(gradients, section, core).astype(jnp.float32)
    grad_proj = proj_grad(order, src_block[0], live[0], frustum_tiles[0], encoded, returned)
    proj_total = total_over_devices(grad_proj, section, core).astype(jnp.float32)

    def up_of(block):
        return jnp.concatenate([head_total[4 * block], head_total[4 * block + 1]], axis=1)

    def down_of(block):
        return jnp.concatenate([head_total[4 * block + 2], head_total[4 * block + 3]], axis=0)

    return (
        prediction[None],
        proj_total.reshape(proj.shape),
        up_of(0),
        down_of(0),
        up_of(1),
        down_of(1),
    )


def solution(mesh):
    placed = (
        P(None, "tile", None),
        P("section", None, None),
        P("section", None, None),
        P(),
        P("tile", None, None, None),
        P("tile", None),
        P("tile", None),
        P("tile", None),
        P(),
        P(),
        P(),
        P(),
        P("section", "tile", None),
    )
    return jax.shard_map(
        on_device,
        mesh=mesh,
        in_specs=placed,
        out_specs=(P("section", "tile", None), P(), P(), P(), P(), P()),
        check_vma=False,
    )
```

```python
import functools
import math

import jax
import jax.numpy as jnp
from jax import lax
from jax.experimental import pallas as pl
from jax.experimental.pallas import tpu as pltpu
from jax.sharding import PartitionSpec as P

eps = 1e-05
gelu_inner = math.sqrt(2.0 / math.pi)
gelu_cubic = 0.044715
mebibyte = 1024 * 1024


def gelu(value):
    inner = gelu_inner * (value + gelu_cubic * (value * value * value))
    half = 0.5 * value
    return half + half * jnp.tanh(inner)


def gelu_and_slope(value):
    square = value * value
    reach = jnp.tanh(gelu_inner * value * (1.0 + gelu_cubic * square))
    half = 0.5 * value
    up_to_one = 0.5 + 0.5 * reach
    slope = up_to_one + half * (1.0 - reach * reach) * (
        gelu_inner + (3.0 * gelu_inner * gelu_cubic) * square
    )
    return (value * up_to_one, slope)


def plain(left, right):
    return jnp.dot(left, right, preferred_element_type=jnp.float32)


def contract_rows(left, right):
    return lax.dot_general(
        left, right, (((0,), (0,)), ((), ())), preferred_element_type=jnp.float32
    )


def against_rows(left, right):
    return lax.dot_general(
        left, right, (((1,), (1,)), ((), ())), preferred_element_type=jnp.float32
    )


def position():
    tile = lax.axis_index("tile")
    return (lax.axis_index("section"), tile, tile % 2, tile // 2 % 2)


def tile_of(number, tile, tiles):
    if tiles != 8:
        return number
    chip = jnp.bitwise_xor(number // 2, tile // 2)
    return 2 * chip + jnp.bitwise_xor(number % 2, tile % 2)


def encode_kernel(
    names,
    counts,
    sources_ref,
    alive_ref,
    table_ref,
    cams_ref,
    own_up_ref,
    own_down_ref,
    proj_ref,
    tiles_ref,
    *rest,
):
    parts = dict(zip(names, rest[: len(names)]))
    rest = rest[len(names) :]
    encoded_ref, targets_ref = rest[:2]
    pieces = rest[2 : 2 + len(counts)]
    state, ups, downs, projected, state_sem, up_sems, down_sems = rest[2 + len(counts) :]
    section, tile, core, zone = position()
    layers, halves, half = ups.shape[:3]
    alone = parts["x_up_own"].shape[0]
    shared = half - 2 * alone
    block_rows = tiles_ref.shape[1]

    load_state = pltpu.make_async_copy(cams_ref.at[section], state, state_sem)
    load_state.start()

    def at_own(kind, name, far, number):
        return (
            (kind, name, 0, alone, pl.multiple_of(zone * alone, 16)),
            (kind, far, number * alone, alone, pl.multiple_of((1 - zone) * alone, 16)),
        )

    where = {
        "x": (
            *at_own("up", "x_up_own", "first_far", 0),
            ("down", "x_pack", 0, half, 0),
            ("up", "x_pack", half, shared, 2 * alone),
        ),
        "y": (
            *at_own("down", "y_down_own", "first_far", 1),
            ("up", "y_pack", 0, half, 0),
            ("down", "y_pack", half, shared, 2 * alone),
        ),
        "d": (
            *at_own("up", "d_up_own", "second_far", 0),
            *at_own("down", "d_down_own", "second_far", 1),
            ("up", "d_shared", 0, shared, 2 * alone),
            ("down", "d_shared", shared, shared, 2 * alone),
        ),
    }
    held = {"up": (ups, up_sems), "down": (downs, down_sems)}

    for layer in range(layers):
        for number, relation in enumerate(("own", "x", "y", "d")):

            @pl.when(jnp.bitwise_xor(section, layer) == number)
            def load(layer=layer, relation=relation):
                if relation == "own":
                    for at in range(halves):
                        pltpu.make_async_copy(
                            own_up_ref.at[:, pl.ds(at * half, half)],
                            ups.at[layer, at],
                            up_sems.at[layer],
                        ).start()
                        pltpu.make_async_copy(
                            own_down_ref.at[pl.ds(at * half, half)],
                            downs.at[layer, at],
                            down_sems.at[layer],
                        ).start()
                    return
                for side, at in (("", core), ("other_", 1 - core)):
                    for kind, name, first, count, to in where[relation]:
                        kept, sems = held[kind]
                        pltpu.make_async_copy(
                            parts[side + name].at[pl.ds(first, count)],
                            kept.at[layer, at, pl.ds(to, count)],
                            sems.at[layer],
                        ).start()

    load_state.wait()
    for layer in range(layers):
        widened = state[...].astype(jnp.float32)
        scaling = lax.rsqrt(jnp.mean(widened * widened, axis=-1, keepdims=True) + eps)
        normed = (widened * scaling).astype(jnp.bfloat16)
        pltpu.make_async_copy(ups.at[layer], ups.at[layer], up_sems.at[layer]).wait()
        pltpu.make_async_copy(downs.at[layer], downs.at[layer], down_sems.at[layer]).wait()
        total = widened
        for at in range(halves):
            hidden = gelu(plain(normed, ups[layer, at])).astype(jnp.bfloat16)
            total = total + plain(hidden, downs[layer, at])
        state[...] = total.astype(jnp.bfloat16)
    encoded_ref[...] = state[...]
    projected[...] = plain(state[...], proj_ref[...]).astype(jnp.bfloat16)

    number = 0
    for ref, count in zip(pieces, counts):

        def slot(at, carry, ref=ref, number=number):
            tile_at = tile_of(number + at, tile, tiles_ref.shape[0])
            first = pl.multiple_of(sources_ref[tile_at] * block_rows, block_rows)
            piece = plain(tiles_ref[tile_at], projected[pl.ds(first, block_rows)])
            piece = piece * alive_ref[tile_at].astype(jnp.float32)
            ref[at] = piece.astype(jnp.bfloat16)
            targets_ref[number + at] = table_ref[jnp.bitwise_xor(tile_at, tile), tile]
            return carry

        lax.fori_loop(0, count, slot, 0, unroll=count <= 8)
        number += count


def encode(
    sources, alive, table, cams, own_up, own_down, proj, tiles, parts, counts
):
    names = tuple(parts)
    tokens, width = cams.shape[1:]
    hidden = own_up.shape[1]
    layers = cams.shape[0]
    half = hidden // 2
    block_rows = tiles.shape[1]
    channels = proj.shape[1]
    smem = pl.BlockSpec(memory_space=pltpu.SMEM)
    vmem = pl.BlockSpec(memory_space=pltpu.VMEM)
    hbm = pl.BlockSpec(memory_space=pl.ANY)
    return pl.pallas_call(
        functools.partial(encode_kernel, names, counts),
        out_shape=(
            jax.ShapeDtypeStruct((tokens, width), jnp.bfloat16),
            jax.ShapeDtypeStruct(sources.shape, jnp.int32),
        )
        + tuple(
            jax.ShapeDtypeStruct((count, block_rows, channels), jnp.bfloat16) for count in counts
        ),
        in_specs=[smem] * 3 + [hbm] * 3 + [vmem] * 2 + [hbm] * len(names),
        out_specs=(vmem, smem) + (vmem,) * len(counts),
        scratch_shapes=[
            pltpu.VMEM((tokens, width), jnp.bfloat16),
            pltpu.VMEM((layers, 2, width, half), jnp.bfloat16),
            pltpu.VMEM((layers, 2, half, width), jnp.bfloat16),
            pltpu.VMEM((tokens, channels), jnp.bfloat16),
            pltpu.SemaphoreType.DMA,
            pltpu.SemaphoreType.DMA((layers,)),
            pltpu.SemaphoreType.DMA((layers,)),
        ],
        compiler_params=pltpu.CompilerParams(vmem_limit_bytes=50 * mebibyte),
        name="encode",
    )(sources, alive, table, cams, own_up, own_down, proj, tiles, *parts.values())


def heads_kernel(
    counts,
    back_counts,
    scale_factor,
    targets_ref,
    render_up_ref,
    render_down_ref,
    decode_up_ref,
    decode_down_ref,
    pred_grad_ref,
    *rest,
):
    arrived = rest[: len(counts)]
    prediction_ref, gradients_ref = rest[len(counts) : len(counts) + 2]
    returns = rest[len(counts) + 2 : -7]
    grid = rest[-7]
    sems = rest[-1]
    loads = [
        pltpu.make_async_copy(source, held, sems.at[at])
        for at, (source, held) in enumerate(
            zip(
                (render_up_ref, render_down_ref, decode_up_ref, decode_down_ref, pred_grad_ref),
                rest[-6:-1],
            )
        )
    ]
    for load in loads:
        load.start()
    render_up_ref, render_down_ref, decode_up_ref, decode_down_ref, pred_grad_ref = rest[-6:-1]
    block_rows = arrived[0].shape[1]
    rows = grid.shape[0]

    grid[...] = jnp.zeros_like(grid)
    number = 0
    for ref, count in zip(arrived, counts):

        def add(at, carry, ref=ref, number=number):
            first = pl.multiple_of(targets_ref[number + at] * block_rows, block_rows)
            grid[pl.ds(first, block_rows)] += ref[at].astype(jnp.float32)
            return carry

        lax.fori_loop(0, count, add, 0, unroll=count <= 8)
        number += count

    for load in loads:
        load.wait()
    weights = ((render_up_ref, render_down_ref), (decode_up_ref, decode_down_ref))
    state = grid[...]
    stored = []
    for w_up, w_down in weights:
        scaling = lax.rsqrt(jnp.mean(state * state, axis=-1, keepdims=True) + eps)
        normed = (state * scaling).astype(jnp.bfloat16)
        value, slope = gelu_and_slope(plain(normed, w_up[...]))
        hidden = value.astype(jnp.bfloat16)
        stored.append((state, scaling, normed, slope, hidden))
        state = state + plain(hidden, w_down[...])
    prediction_ref[...] = state.astype(jnp.bfloat16)

    grad_state = pred_grad_ref[...].astype(jnp.float32) * scale_factor
    width = gradients_ref.shape[-1]
    for block in (1, 0):
        state, scaling, normed, slope, hidden = stored[block]
        w_up, w_down = weights[block]
        rounded = grad_state.astype(jnp.bfloat16)
        grad_down = contract_rows(hidden, rounded).astype(jnp.bfloat16)
        grad_pre = (against_rows(rounded, w_down[...]) * slope).astype(jnp.bfloat16)
        grad_up = contract_rows(normed, grad_pre).astype(jnp.bfloat16)
        gradients_ref[4 * block] = grad_up[:, :width]
        gradients_ref[4 * block + 1] = grad_up[:, width:]
        gradients_ref[4 * block + 2] = grad_down[:width]
        gradients_ref[4 * block + 3] = grad_down[width:]
        grad_normed = against_rows(grad_pre, w_up[...])
        unit_rows = state * scaling
        grad_state = grad_state + scaling * (
            grad_normed - unit_rows * jnp.mean(grad_normed * unit_rows, axis=-1, keepdims=True)
        )
    grid[...] = grad_state
    number = 0
    for ref, count in zip(returns, back_counts):

        def give(at, carry, ref=ref, number=number):
            first = pl.multiple_of(targets_ref[number + at] * block_rows, block_rows)
            ref[at] = grid[pl.ds(first, block_rows)].astype(jnp.bfloat16)
            return carry

        lax.fori_loop(0, count, give, 0, unroll=count <= 8)
        number += count


def heads(targets, weights, pred_grad, arrived, counts, back_counts, scale_factor):
    rows, channels = pred_grad.shape
    smem = pl.BlockSpec(memory_space=pltpu.SMEM)
    vmem = pl.BlockSpec(memory_space=pltpu.VMEM)
    block_rows = arrived[0].shape[1]
    return pl.pallas_call(
        functools.partial(heads_kernel, counts, back_counts, scale_factor),
        out_shape=(
            jax.ShapeDtypeStruct((rows, channels), jnp.bfloat16),
            jax.ShapeDtypeStruct((8, channels, channels), jnp.bfloat16),
        )
        + tuple(
            jax.ShapeDtypeStruct((count, block_rows, channels), jnp.bfloat16)
            for count in back_counts
        ),
        in_specs=[smem] + [pl.BlockSpec(memory_space=pl.ANY)] * 5 + [vmem] * len(arrived),
        out_specs=(vmem,) * (2 + len(back_counts)),
        scratch_shapes=[
            pltpu.VMEM((rows, channels), jnp.float32),
            *[pltpu.VMEM(weight.shape, weight.dtype) for weight in weights],
            pltpu.VMEM(pred_grad.shape, pred_grad.dtype),
            pltpu.SemaphoreType.DMA((5,)),
        ],
        compiler_params=pltpu.CompilerParams(vmem_limit_bytes=50 * mebibyte),
        name="heads",
    )(targets, *weights, pred_grad, *arrived)


def proj_grad_kernel(
    counts, sources_ref, alive_ref, tiles_ref, encoded_ref, *rest
):
    returned = rest[: len(counts)]
    gradient_ref = rest[len(counts)]
    (rows,) = rest[len(counts) + 1 :]
    block_rows = tiles_ref.shape[1]
    rows[...] = jnp.zeros_like(rows)
    number = 0
    for ref, count in zip(returned, counts):

        def add(at, carry, ref=ref, number=number):
            slot = tile_of(number + at, lax.axis_index("tile"), tiles_ref.shape[0])
            first = pl.multiple_of(sources_ref[slot] * block_rows, block_rows)
            product = contract_rows(tiles_ref[slot], ref[at])
            rows[pl.ds(first, block_rows)] += product * alive_ref[slot].astype(jnp.float32)
            return carry

        lax.fori_loop(0, count, add, 0, unroll=count <= 8)
        number += count
    total = contract_rows(encoded_ref[...], rows[...].astype(jnp.bfloat16))
    gradient_ref[...] = total.astype(jnp.bfloat16).reshape(gradient_ref.shape)


def proj_grad(sources, alive, tiles, encoded, returned, counts):
    tokens, width = encoded.shape
    channels = returned[0].shape[-1]
    smem = pl.BlockSpec(memory_space=pltpu.SMEM)
    vmem = pl.BlockSpec(memory_space=pltpu.VMEM)
    return pl.pallas_call(
        functools.partial(proj_grad_kernel, counts),
        out_shape=jax.ShapeDtypeStruct((8, width // 8, channels), jnp.bfloat16),
        in_specs=[smem] * 2 + [vmem] * (2 + len(returned)),
        out_specs=vmem,
        scratch_shapes=[pltpu.VMEM((tokens, channels), jnp.float32)],
        compiler_params=pltpu.CompilerParams(vmem_limit_bytes=16 * mebibyte),
        name="proj_grad",
    )(sources, alive, tiles, encoded, *returned)


def to_section(array, flip):
    count = lax.axis_size("section")
    return lax.ppermute(array, "section", [(at, at ^ flip) for at in range(count)])


def to_tile(array, flip):
    count = lax.axis_size("tile")
    return lax.ppermute(array, "tile", [(at, at ^ flip) for at in range(count)])


def rows_from(array, first, count):
    return lax.dynamic_slice_in_dim(array, first, count, 0)


def cut_kernel(plan, up_ref, down_ref, *rest):
    outputs, sems = rest[:-1], rest[-1]
    _, _, core, zone = position()
    half = down_ref.shape[0] // 2
    copies = []
    for number, (kind, first, step, count, to) in enumerate(plan[0]):
        start = pl.multiple_of(first + step * zone, 16)
        if kind == "up":
            source = up_ref.at[pl.ds(start, count), pl.ds(pl.multiple_of(core * half, 128), half)]
        else:
            source = down_ref.at[pl.ds(pl.multiple_of(core * half + start, 16), count)]
        output, row = to
        copies.append(
            pltpu.make_async_copy(
                source, outputs[output].at[pl.ds(row, count)], sems.at[number]
            )
        )
    for copy in copies:
        copy.start()
    for copy in copies:
        copy.wait()


def cut(up, down, plan, rows):
    width = down.shape[1]
    hbm = pl.BlockSpec(memory_space=pl.ANY)
    vmem = pl.BlockSpec(memory_space=pltpu.VMEM)
    return pl.pallas_call(
        functools.partial(cut_kernel, (plan,)),
        out_shape=tuple(jax.ShapeDtypeStruct((count, width), up.dtype) for count in rows),
        in_specs=[hbm, hbm],
        out_specs=(vmem,) * len(rows),
        scratch_shapes=[pltpu.SemaphoreType.DMA((len(plan),))],
        compiler_params=pltpu.CompilerParams(vmem_limit_bytes=60 * mebibyte),
        name="cut",
    )(up, down)


def gather_layers(own_up, own_down, dst_block):
    half = own_down.shape[0] // 2
    shared = half // 8 // 16 * 16
    alone = (half - shared) // 2
    x_up, y_down = cut(
        own_up,
        own_down,
        (("up", 0, alone, alone, (0, 0)), ("down", 0, alone, alone, (1, 0))),
        (alone, alone),
    )
    down_pack, up_pack, both_shared = cut(
        own_up,
        own_down,
        (
            ("down", 0, 0, half, (0, 0)),
            ("up", 2 * alone, 0, shared, (0, half)),
            ("up", 0, 0, half, (1, 0)),
            ("down", 2 * alone, 0, shared, (1, half)),
            ("up", 2 * alone, 0, shared, (2, 0)),
            ("down", 2 * alone, 0, shared, (2, shared)),
        ),
        (half + shared, half + shared, 2 * shared),
    )
    x_up = to_section(x_up, 1)
    y_down = to_section(y_down, 2)
    table, both_shared = lax.optimization_barrier((dst_block, both_shared))
    flip = 1
    while flip < lax.axis_size("tile"):
        table = jnp.concatenate([table, to_tile(table, flip)])
        flip *= 2
    x_up, y_down, both_shared, table = lax.optimization_barrier(
        (x_up, y_down, both_shared, table)
    )
    d_down = to_section(y_down, 1)
    d_up = to_section(x_up, 2)
    first_far = to_tile(jnp.concatenate([x_up, y_down]), 2)
    d_shared = to_section(both_shared, 3)
    d_up, d_down, down_pack, up_pack = lax.optimization_barrier(
        (d_up, d_down, down_pack, up_pack)
    )
    first_far, second_sent = lax.optimization_barrier(
        (first_far, jnp.concatenate([d_up, d_down]))
    )
    second_far = to_tile(second_sent, 2)
    x_pack = to_section(down_pack, 1)
    y_pack = to_section(up_pack, 2)
    x_pack, y_pack, second_far = lax.optimization_barrier((x_pack, y_pack, second_far))
    parts = {
        "x_up_own": x_up,
        "y_down_own": y_down,
        "d_shared": d_shared,
        "first_far": first_far,
        "d_up_own": d_up,
        "d_down_own": d_down,
        "x_pack": x_pack,
        "y_pack": y_pack,
        "second_far": second_far,
    }
    parts.update({"other_" + name: to_tile(part, 1) for name, part in parts.items()})
    return parts, table


def add_up(left, *others):
    total = left.astype(jnp.float32)
    for other in others:
        total = total + other.astype(jnp.float32)
    return total.astype(jnp.bfloat16)


def section_share(array, section, core):
    count = lax.axis_size("section")
    mine = rows_from(array, core * count, count)
    others = rows_from(array, (1 - core) * count, count)
    mine = add_up(mine, to_tile(others, 1))

    def pick(number):
        return lax.dynamic_index_in_dim(mine, number, 0, keepdims=False)

    return (pick(section), *[to_section(pick(section ^ flip), flip) for flip in (3, 1, 2)])


def chips_shares(share):
    chips = lax.axis_size("tile") // 2
    if chips == 4:
        return (share, *[to_tile(share, 2 * flip) for flip in (2, 3, 1)])
    groups = [[2 * chip + side for chip in range(chips)] for side in (0, 1)]
    return (lax.psum(share, "tile", axis_index_groups=groups),)


def section_shares(share):
    return (share, *[to_section(share, flip) for flip in (1, 2, 3)])


def with_other_core(shares):
    gathered = jnp.stack(shares)
    return (gathered, to_tile(gathered, 1))


def unpack_kernel(gathered_ref, swapped_ref, *outputs):
    section, _, core, _ = position()
    count, rows, columns = gathered_ref.shape
    for side in range(2):
        for number in range(count):
            at = jnp.bitwise_xor(section, number)
            values = jnp.where(
                core == side,
                gathered_ref[at].astype(jnp.float32),
                swapped_ref[at].astype(jnp.float32),
            )
            if len(outputs) == 1:
                outputs[0][pl.ds((side * count + number) * rows, rows)] = values
            elif number < 2:
                outputs[2 * side][:, pl.ds(number * columns, columns)] = values
            else:
                outputs[2 * side + 1][pl.ds((number - 2) * rows, rows)] = values


def unpack(gathered, swapped, shapes):
    vmem = pl.BlockSpec(memory_space=pltpu.VMEM)
    return pl.pallas_call(
        unpack_kernel,
        out_shape=tuple(jax.ShapeDtypeStruct(shape, jnp.float32) for shape in shapes),
        in_specs=[vmem, vmem],
        out_specs=(vmem,) * len(shapes),
        compiler_params=pltpu.CompilerParams(vmem_limit_bytes=16 * mebibyte),
        name="unpack",
    )(gathered, swapped)


def on_device(
    cams,
    vit_up,
    vit_down,
    proj,
    frustum_tiles,
    src_block,
    dst_block,
    live,
    render_up,
    render_down,
    decode_up,
    decode_down,
    pred_grad,
):
    section, _, core, _ = position()
    tile_count = lax.axis_size("tile")
    micro_count = cams.shape[0]
    small = tile_count == 8
    if small:
        pairs = (2, 2, 2, 2)
        singles = (1,) * 8
    else:
        pairs = singles = (tile_count,)

    def cross(sent):
        if not small:
            return [lax.all_to_all(sent[0], "tile", split_axis=0, concat_axis=0, tiled=True)]
        moved = {0: sent[0]}
        for flip in (2, 3, 1):
            moved[flip] = to_tile(sent[flip], 2 * flip)
        return [moved[flip] for flip in range(4)]

    def over(moved):
        if not small:
            return moved
        found = []
        for part in moved:
            found += [part, to_tile(part[1:], 1)]
        return found

    parts, table = gather_layers(vit_up[0], vit_down[0], dst_block)
    encoded, targets, *pieces = encode(
        src_block[0], live[0], table, cams, vit_up[0], vit_down[0], proj,
        frustum_tiles[0], parts, pairs,
    )
    arrived = over(cross(pieces))

    scale_factor = 1.0 / math.sqrt(micro_count * pred_grad.shape[1] * tile_count)
    weights = (render_up, render_down, decode_up, decode_down)
    prediction, gradients, *returns = heads(
        targets, weights, pred_grad[0], arrived, singles, pairs, scale_factor
    )

    moved = cross(returns)
    head_shares = section_share(gradients, section, core)
    moved, head_shares = lax.optimization_barrier((moved, head_shares))
    returned = over(moved)
    head_shares = chips_shares(add_up(*head_shares))
    grad_proj = proj_grad(
        src_block[0], live[0], frustum_tiles[0], encoded, returned, singles
    )
    proj_shares = section_share(grad_proj, section, core)
    proj_shares = chips_shares(add_up(*proj_shares))
    head_shares = section_shares(add_up(*head_shares))
    proj_shares = section_shares(add_up(*proj_shares))
    head_shares = with_other_core(head_shares)
    grads = unpack(
        *head_shares,
        (render_up.shape, render_down.shape, decode_up.shape, decode_down.shape),
    )
    (grad_proj,) = unpack(*with_other_core(proj_shares), (proj.shape,))
    return (prediction[None], grad_proj, *grads)


def solution(mesh):
    placed = (
        P(None, "tile", None),
        P("section", None, None),
        P("section", None, None),
        P(),
        P("tile", None, None, None),
        P("tile", None),
        P("tile", None),
        P("tile", None),
        P(),
        P(),
        P(),
        P(),
        P("section", "tile", None),
    )
    return jax.shard_map(
        on_device,
        mesh=mesh,
        in_specs=placed,
        out_specs=(P("section", "tile", None), P(), P(), P(), P(), P()),
        check_vma=False,
    )
```

```python
import functools
import math

import jax
import jax.numpy as jnp
from jax import lax
from jax.experimental import pallas as pl
from jax.experimental.pallas import tpu as pltpu
from jax.sharding import PartitionSpec as P

eps = 1e-05
gelu_inner = math.sqrt(2.0 / math.pi)
gelu_cubic = 0.044715
mebibyte = 1024 * 1024


def gelu(value):
    inner = gelu_inner * (value + gelu_cubic * (value * value * value))
    half = 0.5 * value
    return half + half * jnp.tanh(inner)


def gelu_and_slope(value):
    square = value * value
    reach = jnp.tanh(gelu_inner * value * (1.0 + gelu_cubic * square))
    half = 0.5 * value
    up_to_one = 0.5 + 0.5 * reach
    slope = up_to_one + half * (1.0 - reach * reach) * (
        gelu_inner + (3.0 * gelu_inner * gelu_cubic) * square
    )
    return (value * up_to_one, slope)


def plain(left, right):
    return jnp.dot(left, right, preferred_element_type=jnp.float32)


def contract_rows(left, right):
    return lax.dot_general(
        left, right, (((0,), (0,)), ((), ())), preferred_element_type=jnp.float32
    )


def against_rows(left, right):
    return lax.dot_general(
        left, right, (((1,), (1,)), ((), ())), preferred_element_type=jnp.float32
    )


def position():
    tile = lax.axis_index("tile")
    return (lax.axis_index("section"), tile, tile % 2, tile // 2 % 2)


def tile_of(number, tile, tiles):
    if tiles != 8:
        return number
    chip = jnp.bitwise_xor(number // 2, tile // 2)
    return 2 * chip + jnp.bitwise_xor(number % 2, tile % 2)


def encode_kernel(
    names,
    counts,
    sources_ref,
    alive_ref,
    table_ref,
    cams_ref,
    own_up_ref,
    own_down_ref,
    proj_ref,
    tiles_ref,
    *rest,
):
    parts = dict(zip(names, rest[: len(names)]))
    rest = rest[len(names) :]
    encoded_ref, targets_ref = rest[:2]
    pieces = rest[2 : 2 + len(counts)]
    state, ups, downs, projected, state_sem, up_sems, down_sems = rest[2 + len(counts) :]
    section, tile, core, zone = position()
    layers, halves, half = ups.shape[:3]
    window = parts["x_up_window"].shape[0]
    alone = half - window
    block_rows = tiles_ref.shape[1]

    load_state = pltpu.make_async_copy(cams_ref.at[section], state, state_sem)
    load_state.start()

    def windowed(kind, name, far, number):
        return (
            (kind, name, 0, window, pl.multiple_of(zone * alone, 16)),
            (kind, far, number * alone, alone, pl.multiple_of((1 - zone) * window, 16)),
        )

    where = {
        "x": (*windowed("up", "x_up_window", "first_far", 0), ("down", "x_down", 0, half, 0)),
        "y": (*windowed("down", "y_down_window", "first_far", 1), ("up", "y_up", 0, half, 0)),
        "d": (
            *windowed("up", "d_up_window", "second_far", 0),
            *windowed("down", "d_down_window", "second_far", 1),
        ),
    }
    held = {"up": (ups, up_sems), "down": (downs, down_sems)}

    for layer in range(layers):
        for number, relation in enumerate(("own", "x", "y", "d")):

            @pl.when(jnp.bitwise_xor(section, layer) == number)
            def load(layer=layer, relation=relation):
                if relation == "own":
                    for at in range(halves):
                        pltpu.make_async_copy(
                            own_up_ref.at[:, pl.ds(at * half, half)],
                            ups.at[layer, at],
                            up_sems.at[layer],
                        ).start()
                        pltpu.make_async_copy(
                            own_down_ref.at[pl.ds(at * half, half)],
                            downs.at[layer, at],
                            down_sems.at[layer],
                        ).start()
                    return
                for side, at in (("", core), ("other_", 1 - core)):
                    for kind, name, first, count, to in where[relation]:
                        kept, sems = held[kind]
                        pltpu.make_async_copy(
                            parts[side + name].at[pl.ds(first, count)],
                            kept.at[layer, at, pl.ds(to, count)],
                            sems.at[layer],
                        ).start()

    load_state.wait()
    for layer in range(layers):
        widened = state[...].astype(jnp.float32)
        scaling = lax.rsqrt(jnp.mean(widened * widened, axis=-1, keepdims=True) + eps)
        normed = (widened * scaling).astype(jnp.bfloat16)
        pltpu.make_async_copy(ups.at[layer], ups.at[layer], up_sems.at[layer]).wait()
        pltpu.make_async_copy(downs.at[layer], downs.at[layer], down_sems.at[layer]).wait()
        hidden = [
            gelu(plain(normed, ups[layer, at])).astype(jnp.bfloat16) for at in range(halves)
        ]
        total = widened
        for at in range(halves):
            total = total + plain(hidden[at], downs[layer, at])
        state[...] = total.astype(jnp.bfloat16)
    encoded_ref[...] = state[...]
    projected[...] = plain(state[...], proj_ref[...]).astype(jnp.bfloat16)

    number = 0
    for ref, count in zip(pieces, counts):

        def slot(at, carry, ref=ref, number=number):
            tile_at = tile_of(number + at, tile, tiles_ref.shape[0])
            first = pl.multiple_of(sources_ref[tile_at] * block_rows, block_rows)
            piece = plain(tiles_ref[tile_at], projected[pl.ds(first, block_rows)])
            piece = piece * alive_ref[tile_at].astype(jnp.float32)
            ref[at] = piece.astype(jnp.bfloat16)
            targets_ref[number + at] = table_ref[jnp.bitwise_xor(tile_at, tile), tile]
            return carry

        lax.fori_loop(0, count, slot, 0, unroll=count <= 8)
        number += count


def encode(
    sources, alive, table, cams, own_up, own_down, proj, tiles, parts, counts
):
    names = tuple(parts)
    tokens, width = cams.shape[1:]
    hidden = own_up.shape[1]
    layers = cams.shape[0]
    half = hidden // 2
    block_rows = tiles.shape[1]
    channels = proj.shape[1]
    smem = pl.BlockSpec(memory_space=pltpu.SMEM)
    vmem = pl.BlockSpec(memory_space=pltpu.VMEM)
    hbm = pl.BlockSpec(memory_space=pl.ANY)
    return pl.pallas_call(
        functools.partial(encode_kernel, names, counts),
        out_shape=(
            jax.ShapeDtypeStruct((tokens, width), jnp.bfloat16),
            jax.ShapeDtypeStruct(sources.shape, jnp.int32),
        )
        + tuple(
            jax.ShapeDtypeStruct((count, block_rows, channels), jnp.bfloat16) for count in counts
        ),
        in_specs=[smem] * 3 + [hbm] * 3 + [vmem] * 2 + [hbm] * len(names),
        out_specs=(vmem, smem) + (vmem,) * len(counts),
        scratch_shapes=[
            pltpu.VMEM((tokens, width), jnp.bfloat16),
            pltpu.VMEM((layers, 2, width, half), jnp.bfloat16),
            pltpu.VMEM((layers, 2, half, width), jnp.bfloat16),
            pltpu.VMEM((tokens, channels), jnp.bfloat16),
            pltpu.SemaphoreType.DMA,
            pltpu.SemaphoreType.DMA((layers,)),
            pltpu.SemaphoreType.DMA((layers,)),
        ],
        compiler_params=pltpu.CompilerParams(vmem_limit_bytes=50 * mebibyte),
        name="encode",
    )(sources, alive, table, cams, own_up, own_down, proj, tiles, *parts.values())


def heads_kernel(
    counts,
    back_counts,
    scale_factor,
    targets_ref,
    render_up_ref,
    render_down_ref,
    decode_up_ref,
    decode_down_ref,
    pred_grad_ref,
    *rest,
):
    arrived = rest[: len(counts)]
    prediction_ref, gradients_ref = rest[len(counts) : len(counts) + 2]
    returns = rest[len(counts) + 2 : -7]
    grid = rest[-7]
    sems = rest[-1]
    loads = [
        pltpu.make_async_copy(source, held, sems.at[at])
        for at, (source, held) in enumerate(
            zip(
                (render_up_ref, render_down_ref, decode_up_ref, decode_down_ref, pred_grad_ref),
                rest[-6:-1],
            )
        )
    ]
    for load in loads:
        load.start()
    render_up_ref, render_down_ref, decode_up_ref, decode_down_ref, pred_grad_ref = rest[-6:-1]
    block_rows = arrived[0].shape[1]
    rows = grid.shape[0]

    grid[...] = jnp.zeros_like(grid)
    number = 0
    for ref, count in zip(arrived, counts):

        def add(at, carry, ref=ref, number=number):
            first = pl.multiple_of(targets_ref[number + at] * block_rows, block_rows)
            grid[pl.ds(first, block_rows)] += ref[at].astype(jnp.float32)
            return carry

        lax.fori_loop(0, count, add, 0, unroll=count <= 8)
        number += count

    for load in loads:
        load.wait()
    weights = ((render_up_ref, render_down_ref), (decode_up_ref, decode_down_ref))
    state = grid[...]
    stored = []
    for w_up, w_down in weights:
        scaling = lax.rsqrt(jnp.mean(state * state, axis=-1, keepdims=True) + eps)
        normed = (state * scaling).astype(jnp.bfloat16)
        value, slope = gelu_and_slope(plain(normed, w_up[...]))
        hidden = value.astype(jnp.bfloat16)
        stored.append((state, scaling, normed, slope, hidden))
        state = state + plain(hidden, w_down[...])
    prediction_ref[...] = state.astype(jnp.bfloat16)

    grad_state = pred_grad_ref[...].astype(jnp.float32) * scale_factor
    width = gradients_ref.shape[-1]
    for block in (1, 0):
        state, scaling, normed, slope, hidden = stored[block]
        w_up, w_down = weights[block]
        rounded = grad_state.astype(jnp.bfloat16)
        grad_down = contract_rows(hidden, rounded).astype(jnp.bfloat16)
        grad_pre = (against_rows(rounded, w_down[...]) * slope).astype(jnp.bfloat16)
        grad_up = contract_rows(normed, grad_pre).astype(jnp.bfloat16)
        gradients_ref[4 * block] = grad_up[:, :width]
        gradients_ref[4 * block + 1] = grad_up[:, width:]
        gradients_ref[4 * block + 2] = grad_down[:width]
        gradients_ref[4 * block + 3] = grad_down[width:]
        grad_normed = against_rows(grad_pre, w_up[...])
        unit_rows = state * scaling
        grad_state = grad_state + scaling * (
            grad_normed - unit_rows * jnp.mean(grad_normed * unit_rows, axis=-1, keepdims=True)
        )
    grid[...] = grad_state
    number = 0
    for ref, count in zip(returns, back_counts):

        def give(at, carry, ref=ref, number=number):
            first = pl.multiple_of(targets_ref[number + at] * block_rows, block_rows)
            ref[at] = grid[pl.ds(first, block_rows)].astype(jnp.bfloat16)
            return carry

        lax.fori_loop(0, count, give, 0, unroll=count <= 8)
        number += count


def heads(targets, weights, pred_grad, arrived, counts, back_counts, scale_factor):
    rows, channels = pred_grad.shape
    smem = pl.BlockSpec(memory_space=pltpu.SMEM)
    vmem = pl.BlockSpec(memory_space=pltpu.VMEM)
    block_rows = arrived[0].shape[1]
    return pl.pallas_call(
        functools.partial(heads_kernel, counts, back_counts, scale_factor),
        out_shape=(
            jax.ShapeDtypeStruct((rows, channels), jnp.bfloat16),
            jax.ShapeDtypeStruct((8, channels, channels), jnp.bfloat16),
        )
        + tuple(
            jax.ShapeDtypeStruct((count, block_rows, channels), jnp.bfloat16)
            for count in back_counts
        ),
        in_specs=[smem] + [pl.BlockSpec(memory_space=pl.ANY)] * 5 + [vmem] * len(arrived),
        out_specs=(vmem,) * (2 + len(back_counts)),
        scratch_shapes=[
            pltpu.VMEM((rows, channels), jnp.float32),
            *[pltpu.VMEM(weight.shape, weight.dtype) for weight in weights],
            pltpu.VMEM(pred_grad.shape, pred_grad.dtype),
            pltpu.SemaphoreType.DMA((5,)),
        ],
        compiler_params=pltpu.CompilerParams(vmem_limit_bytes=50 * mebibyte),
        name="heads",
    )(targets, *weights, pred_grad, *arrived)


def proj_grad_kernel(
    counts, sources_ref, alive_ref, tiles_ref, encoded_ref, *rest
):
    returned = rest[: len(counts)]
    gradient_ref = rest[len(counts)]
    (rows,) = rest[len(counts) + 1 :]
    block_rows = tiles_ref.shape[1]
    rows[...] = jnp.zeros_like(rows)
    number = 0
    for ref, count in zip(returned, counts):

        def add(at, carry, ref=ref, number=number):
            slot = tile_of(number + at, lax.axis_index("tile"), tiles_ref.shape[0])
            first = pl.multiple_of(sources_ref[slot] * block_rows, block_rows)
            product = contract_rows(tiles_ref[slot], ref[at])
            rows[pl.ds(first, block_rows)] += product * alive_ref[slot].astype(jnp.float32)
            return carry

        lax.fori_loop(0, count, add, 0, unroll=count <= 8)
        number += count
    total = contract_rows(encoded_ref[...], rows[...].astype(jnp.bfloat16))
    gradient_ref[...] = total.astype(jnp.bfloat16).reshape(gradient_ref.shape)


def proj_grad(sources, alive, tiles, encoded, returned, counts):
    tokens, width = encoded.shape
    channels = returned[0].shape[-1]
    smem = pl.BlockSpec(memory_space=pltpu.SMEM)
    vmem = pl.BlockSpec(memory_space=pltpu.VMEM)
    return pl.pallas_call(
        functools.partial(proj_grad_kernel, counts),
        out_shape=jax.ShapeDtypeStruct((8, width // 8, channels), jnp.bfloat16),
        in_specs=[smem] * 2 + [vmem] * (2 + len(returned)),
        out_specs=vmem,
        scratch_shapes=[pltpu.VMEM((tokens, channels), jnp.float32)],
        compiler_params=pltpu.CompilerParams(vmem_limit_bytes=16 * mebibyte),
        name="proj_grad",
    )(sources, alive, tiles, encoded, *returned)


def to_section(array, flip):
    count = lax.axis_size("section")
    return lax.ppermute(array, "section", [(at, at ^ flip) for at in range(count)])


def to_tile(array, flip):
    count = lax.axis_size("tile")
    return lax.ppermute(array, "tile", [(at, at ^ flip) for at in range(count)])


def rows_from(array, first, count):
    return lax.dynamic_slice_in_dim(array, first, count, 0)


def cut_kernel(plan, up_ref, down_ref, *rest):
    outputs, sems = rest[:-1], rest[-1]
    _, _, core, zone = position()
    half = down_ref.shape[0] // 2
    copies = []
    for number, (kind, first, step, count, to) in enumerate(plan[0]):
        start = pl.multiple_of(first + step * zone, 16)
        if kind == "up":
            source = up_ref.at[pl.ds(start, count), pl.ds(pl.multiple_of(core * half, 128), half)]
        else:
            source = down_ref.at[pl.ds(pl.multiple_of(core * half + start, 16), count)]
        output, row = to
        copies.append(
            pltpu.make_async_copy(
                source, outputs[output].at[pl.ds(row, count)], sems.at[number]
            )
        )
    for copy in copies:
        copy.start()
    for copy in copies:
        copy.wait()


def cut(up, down, plan, rows):
    width = down.shape[1]
    hbm = pl.BlockSpec(memory_space=pl.ANY)
    vmem = pl.BlockSpec(memory_space=pltpu.VMEM)
    return pl.pallas_call(
        functools.partial(cut_kernel, (plan,)),
        out_shape=tuple(jax.ShapeDtypeStruct((count, width), up.dtype) for count in rows),
        in_specs=[hbm, hbm],
        out_specs=(vmem,) * len(rows),
        scratch_shapes=[pltpu.SemaphoreType.DMA((len(plan),))],
        compiler_params=pltpu.CompilerParams(vmem_limit_bytes=60 * mebibyte),
        name="cut",
    )(up, down)


def pick_missing(upper, lower, alone):
    zone = position()[3]
    return jnp.concatenate(
        [
            jnp.where(zone == 0, array[:alone], array[array.shape[0] - alone :])
            for array in (upper, lower)
        ]
    )


def gather_layers(own_up, own_down, dst_block):
    half = own_down.shape[0] // 2
    alone = half * 2 // 5 // 16 * 16
    window = half - alone
    x_up, y_down = cut(
        own_up,
        own_down,
        (("up", 0, alone, window, (0, 0)), ("down", 0, alone, window, (1, 0))),
        (window, window),
    )
    table, x_up = lax.optimization_barrier((dst_block, x_up))
    flip = 1
    while flip < lax.axis_size("tile"):
        table = jnp.concatenate([table, to_tile(table, flip)])
        flip *= 2
    table, own_up, own_down = lax.optimization_barrier((table, own_up, own_down))
    down, up = cut(
        own_up, own_down, (("down", 0, 0, half, (0, 0)), ("up", 0, 0, half, (1, 0))), (half, half)
    )
    x_up = to_section(x_up, 1)
    y_down = to_section(y_down, 2)
    x_up, y_down, up, down = lax.optimization_barrier((x_up, y_down, up, down))
    d_down = to_section(y_down, 1)
    d_up = to_section(x_up, 2)
    first_far = to_tile(pick_missing(x_up, y_down, alone), 2)
    other_x_up = to_tile(x_up, 1)
    other_y_down = to_tile(y_down, 1)
    other_x_up, other_y_down, down, up = lax.optimization_barrier(
        (other_x_up, other_y_down, down, up)
    )
    x_down = to_section(down, 1)
    y_up = to_section(up, 2)
    first_far, d_up, d_down = lax.optimization_barrier((first_far, d_up, d_down))
    second_far = to_tile(pick_missing(d_up, d_down, alone), 2)
    parts = {"first_far": first_far, "d_up_window": d_up, "d_down_window": d_down}
    parts.update({"other_" + name: to_tile(part, 1) for name, part in parts.items()})
    last = {"x_down": x_down, "y_up": y_up, "second_far": second_far}
    parts, last = lax.optimization_barrier((parts, last))
    parts.update(last)
    parts.update({"other_" + name: to_tile(part, 1) for name, part in last.items()})
    parts.update({"x_up_window": x_up, "y_down_window": y_down})
    parts.update({"other_x_up_window": other_x_up, "other_y_down_window": other_y_down})
    return parts, table


def add_up(left, *others):
    total = left.astype(jnp.float32)
    for other in others:
        total = total + other.astype(jnp.float32)
    return total.astype(jnp.bfloat16)


def section_share(array, section, core):
    count = lax.axis_size("section")
    mine = rows_from(array, core * count, count)
    others = rows_from(array, (1 - core) * count, count)
    mine = add_up(mine, to_tile(others, 1))

    def pick(number):
        return lax.dynamic_index_in_dim(mine, number, 0, keepdims=False)

    return (pick(section), *[to_section(pick(section ^ flip), flip) for flip in (3, 1, 2)])


def chips_total(share):
    flip = 2
    while flip < lax.axis_size("tile"):
        share = add_up(share, to_tile(share, flip))
        flip *= 2
    return share


def section_shares(share):
    return (share, *[to_section(share, flip) for flip in (1, 2, 3)])


def with_other_core(shares):
    gathered = jnp.stack(shares)
    return (gathered, to_tile(gathered, 1))


def unpack_kernel(gathered_ref, swapped_ref, *outputs):
    section, _, core, _ = position()
    count, rows, columns = gathered_ref.shape
    for side in range(2):
        for number in range(count):
            at = jnp.bitwise_xor(section, number)
            values = jnp.where(
                core == side,
                gathered_ref[at].astype(jnp.float32),
                swapped_ref[at].astype(jnp.float32),
            )
            if len(outputs) == 1:
                outputs[0][pl.ds((side * count + number) * rows, rows)] = values
            elif number < 2:
                outputs[2 * side][:, pl.ds(number * columns, columns)] = values
            else:
                outputs[2 * side + 1][pl.ds((number - 2) * rows, rows)] = values


def unpack(gathered, swapped, shapes):
    vmem = pl.BlockSpec(memory_space=pltpu.VMEM)
    return pl.pallas_call(
        unpack_kernel,
        out_shape=tuple(jax.ShapeDtypeStruct(shape, jnp.float32) for shape in shapes),
        in_specs=[vmem, vmem],
        out_specs=(vmem,) * len(shapes),
        compiler_params=pltpu.CompilerParams(vmem_limit_bytes=16 * mebibyte),
        name="unpack",
    )(gathered, swapped)


def on_device(
    cams,
    vit_up,
    vit_down,
    proj,
    frustum_tiles,
    src_block,
    dst_block,
    live,
    render_up,
    render_down,
    decode_up,
    decode_down,
    pred_grad,
):
    section, _, core, _ = position()
    tile_count = lax.axis_size("tile")
    micro_count = cams.shape[0]
    small = tile_count == 8
    if small:
        pairs = (2, 2, 2, 2)
        singles = (1,) * 8
    else:
        pairs = singles = (tile_count,)

    def cross(sent):
        if not small:
            return [lax.all_to_all(sent[0], "tile", split_axis=0, concat_axis=0, tiled=True)]
        over_near = to_tile(sent[0][1:], 1)
        moved = {flip: to_tile(sent[flip], 2 * flip) for flip in (2, 3)}
        over_near, nearest = lax.optimization_barrier((over_near, sent[1]))
        moved[1] = to_tile(nearest, 2)
        return [sent[0], over_near, *[moved[flip] for flip in (1, 2, 3)]]

    def over(moved):
        if not small:
            return moved
        found = moved[:2]
        for part in moved[2:]:
            found += [part, to_tile(part[1:], 1)]
        return found

    parts, table = gather_layers(vit_up[0], vit_down[0], dst_block)
    encoded, targets, *pieces = encode(
        src_block[0], live[0], table, cams, vit_up[0], vit_down[0], proj,
        frustum_tiles[0], parts, pairs,
    )
    arrived = over(cross(pieces))

    scale_factor = 1.0 / math.sqrt(micro_count * pred_grad.shape[1] * tile_count)
    weights = (render_up, render_down, decode_up, decode_down)
    prediction, gradients, *returns = heads(
        targets, weights, pred_grad[0], arrived, singles, pairs, scale_factor
    )

    moved = cross(returns)
    head_shares = section_share(gradients, section, core)
    moved, head_shares = lax.optimization_barrier((moved, head_shares))
    returned = over(moved)
    head_total = chips_total(add_up(*head_shares))
    grad_proj = proj_grad(
        src_block[0], live[0], frustum_tiles[0], encoded, returned, singles
    )
    proj_total = chips_total(add_up(*section_share(grad_proj, section, core)))
    head_shares = with_other_core(section_shares(head_total))
    proj_shares = section_shares(proj_total)
    grads = unpack(
        *head_shares,
        (render_up.shape, render_down.shape, decode_up.shape, decode_down.shape),
    )
    grads, proj_shares = lax.optimization_barrier((grads, with_other_core(proj_shares)))
    (grad_proj,) = unpack(*proj_shares, (proj.shape,))
    return (prediction[None], grad_proj, *grads)


def solution(mesh):
    placed = (
        P(None, "tile", None),
        P("section", None, None),
        P("section", None, None),
        P(),
        P("tile", None, None, None),
        P("tile", None),
        P("tile", None),
        P("tile", None),
        P(),
        P(),
        P(),
        P(),
        P("section", "tile", None),
    )
    return jax.shard_map(
        on_device,
        mesh=mesh,
        in_specs=placed,
        out_specs=(P("section", "tile", None), P(), P(), P(), P(), P()),
        check_vma=False,
    )
```

```python
import functools
import math

import jax
import jax.numpy as jnp
from jax import lax
from jax.experimental import pallas as pl
from jax.experimental.pallas import tpu as pltpu
from jax.sharding import PartitionSpec as P

eps = 1e-05
gelu_inner = math.sqrt(2.0 / math.pi)
gelu_cubic = 0.044715
mebibyte = 1024 * 1024


def gelu(value):
    inner = gelu_inner * (value + gelu_cubic * (value * value * value))
    half = 0.5 * value
    return half + half * jnp.tanh(inner)


def gelu_and_slope(value):
    square = value * value
    reach = jnp.tanh(gelu_inner * value * (1.0 + gelu_cubic * square))
    half = 0.5 * value
    up_to_one = 0.5 + 0.5 * reach
    slope = up_to_one + half * (1.0 - reach * reach) * (
        gelu_inner + (3.0 * gelu_inner * gelu_cubic) * square
    )
    return (value * up_to_one, slope)


def plain(left, right):
    return jnp.dot(left, right, preferred_element_type=jnp.float32)


def contract_rows(left, right):
    return lax.dot_general(
        left, right, (((0,), (0,)), ((), ())), preferred_element_type=jnp.float32
    )


def against_rows(left, right):
    return lax.dot_general(
        left, right, (((1,), (1,)), ((), ())), preferred_element_type=jnp.float32
    )


def position():
    tile = lax.axis_index("tile")
    return (lax.axis_index("section"), tile, tile % 2, tile // 2 % 2)


def tile_of(number, tile, tiles):
    if tiles != 8:
        return number
    chip = jnp.bitwise_xor(number // 2, tile // 2)
    return 2 * chip + jnp.bitwise_xor(number % 2, tile % 2)


def encode_kernel(
    names,
    counts,
    sources_ref,
    alive_ref,
    table_ref,
    cams_ref,
    own_up_ref,
    own_down_ref,
    proj_ref,
    tiles_ref,
    *rest,
):
    parts = dict(zip(names, rest[: len(names)]))
    rest = rest[len(names) :]
    encoded_ref, targets_ref = rest[:2]
    pieces = rest[2 : 2 + len(counts)]
    state, ups, downs, projected, state_sem, up_sems, down_sems = rest[2 + len(counts) :]
    section, tile, core, zone = position()
    layers, halves, half = ups.shape[:3]
    window = parts["x_up_window"].shape[0]
    alone = half - window
    block_rows = tiles_ref.shape[1]

    load_state = pltpu.make_async_copy(cams_ref.at[section], state, state_sem)
    load_state.start()

    def windowed(kind, name, far, number):
        return (
            (kind, name, 0, window, pl.multiple_of(zone * alone, 16)),
            (kind, far, number * alone, alone, pl.multiple_of((1 - zone) * window, 16)),
        )

    where = {
        "x": (*windowed("up", "x_up_window", "first_far", 0), ("down", "x_down", 0, half, 0)),
        "y": (*windowed("down", "y_down_window", "first_far", 1), ("up", "y_up", 0, half, 0)),
        "d": (
            *windowed("up", "d_up_window", "second_far", 0),
            *windowed("down", "d_down_window", "second_far", 1),
        ),
    }
    held = {"up": (ups, up_sems), "down": (downs, down_sems)}

    for layer in range(layers):
        for number, relation in enumerate(("own", "x", "y", "d")):

            @pl.when(jnp.bitwise_xor(section, layer) == number)
            def load(layer=layer, relation=relation):
                if relation == "own":
                    for at in range(halves):
                        pltpu.make_async_copy(
                            own_up_ref.at[:, pl.ds(at * half, half)],
                            ups.at[layer, at],
                            up_sems.at[layer],
                        ).start()
                        pltpu.make_async_copy(
                            own_down_ref.at[pl.ds(at * half, half)],
                            downs.at[layer, at],
                            down_sems.at[layer],
                        ).start()
                    return
                for side, at in (("", core), ("other_", 1 - core)):
                    for kind, name, first, count, to in where[relation]:
                        kept, sems = held[kind]
                        pltpu.make_async_copy(
                            parts[side + name].at[pl.ds(first, count)],
                            kept.at[layer, at, pl.ds(to, count)],
                            sems.at[layer],
                        ).start()

    load_state.wait()
    for layer in range(layers):
        widened = state[...].astype(jnp.float32)
        scaling = lax.rsqrt(jnp.mean(widened * widened, axis=-1, keepdims=True) + eps)
        normed = (widened * scaling).astype(jnp.bfloat16)
        pltpu.make_async_copy(ups.at[layer], ups.at[layer], up_sems.at[layer]).wait()
        pltpu.make_async_copy(downs.at[layer], downs.at[layer], down_sems.at[layer]).wait()
        hidden = [
            gelu(plain(normed, ups[layer, at])).astype(jnp.bfloat16) for at in range(halves)
        ]
        total = widened
        for at in range(halves):
            total = total + plain(hidden[at], downs[layer, at])
        state[...] = total.astype(jnp.bfloat16)
    encoded_ref[...] = state[...]
    projected[...] = plain(state[...], proj_ref[...]).astype(jnp.bfloat16)

    number = 0
    for ref, count in zip(pieces, counts):

        def slot(at, carry, ref=ref, number=number):
            tile_at = tile_of(number + at, tile, tiles_ref.shape[0])
            first = pl.multiple_of(sources_ref[tile_at] * block_rows, block_rows)
            piece = plain(tiles_ref[tile_at], projected[pl.ds(first, block_rows)])
            piece = piece * alive_ref[tile_at].astype(jnp.float32)
            ref[at] = piece.astype(jnp.bfloat16)
            targets_ref[number + at] = table_ref[jnp.bitwise_xor(tile_at, tile), tile]
            return carry

        lax.fori_loop(0, count, slot, 0, unroll=count <= 8)
        number += count


def encode(
    sources, alive, table, cams, own_up, own_down, proj, tiles, parts, counts
):
    names = tuple(parts)
    tokens, width = cams.shape[1:]
    hidden = own_up.shape[1]
    layers = cams.shape[0]
    half = hidden // 2
    block_rows = tiles.shape[1]
    channels = proj.shape[1]
    smem = pl.BlockSpec(memory_space=pltpu.SMEM)
    vmem = pl.BlockSpec(memory_space=pltpu.VMEM)
    hbm = pl.BlockSpec(memory_space=pl.ANY)
    return pl.pallas_call(
        functools.partial(encode_kernel, names, counts),
        out_shape=(
            jax.ShapeDtypeStruct((tokens, width), jnp.bfloat16),
            jax.ShapeDtypeStruct(sources.shape, jnp.int32),
        )
        + tuple(
            jax.ShapeDtypeStruct((count, block_rows, channels), jnp.bfloat16) for count in counts
        ),
        in_specs=[smem] * 3 + [hbm] * 3 + [vmem] * 2 + [hbm] * len(names),
        out_specs=(vmem, smem) + (vmem,) * len(counts),
        scratch_shapes=[
            pltpu.VMEM((tokens, width), jnp.bfloat16),
            pltpu.VMEM((layers, 2, width, half), jnp.bfloat16),
            pltpu.VMEM((layers, 2, half, width), jnp.bfloat16),
            pltpu.VMEM((tokens, channels), jnp.bfloat16),
            pltpu.SemaphoreType.DMA,
            pltpu.SemaphoreType.DMA((layers,)),
            pltpu.SemaphoreType.DMA((layers,)),
        ],
        compiler_params=pltpu.CompilerParams(vmem_limit_bytes=50 * mebibyte),
        name="encode",
    )(sources, alive, table, cams, own_up, own_down, proj, tiles, *parts.values())


def heads_kernel(
    counts,
    back_counts,
    scale_factor,
    targets_ref,
    render_up_ref,
    render_down_ref,
    decode_up_ref,
    decode_down_ref,
    pred_grad_ref,
    *rest,
):
    arrived = rest[: len(counts)]
    prediction_ref, gradients_ref = rest[len(counts) : len(counts) + 2]
    returns = rest[len(counts) + 2 : -7]
    grid = rest[-7]
    sems = rest[-1]
    loads = [
        pltpu.make_async_copy(source, held, sems.at[at])
        for at, (source, held) in enumerate(
            zip(
                (render_up_ref, render_down_ref, decode_up_ref, decode_down_ref, pred_grad_ref),
                rest[-6:-1],
            )
        )
    ]
    for load in loads:
        load.start()
    render_up_ref, render_down_ref, decode_up_ref, decode_down_ref, pred_grad_ref = rest[-6:-1]
    block_rows = arrived[0].shape[1]
    rows = grid.shape[0]

    grid[...] = jnp.zeros_like(grid)
    number = 0
    for ref, count in zip(arrived, counts):

        def add(at, carry, ref=ref, number=number):
            first = pl.multiple_of(targets_ref[number + at] * block_rows, block_rows)
            grid[pl.ds(first, block_rows)] += ref[at].astype(jnp.float32)
            return carry

        lax.fori_loop(0, count, add, 0, unroll=count <= 8)
        number += count

    for load in loads:
        load.wait()
    weights = ((render_up_ref, render_down_ref), (decode_up_ref, decode_down_ref))
    state = grid[...]
    stored = []
    for w_up, w_down in weights:
        scaling = lax.rsqrt(jnp.mean(state * state, axis=-1, keepdims=True) + eps)
        normed = (state * scaling).astype(jnp.bfloat16)
        value, slope = gelu_and_slope(plain(normed, w_up[...]))
        hidden = value.astype(jnp.bfloat16)
        stored.append((state, scaling, normed, slope, hidden))
        state = state + plain(hidden, w_down[...])
    prediction_ref[...] = state.astype(jnp.bfloat16)

    grad_state = pred_grad_ref[...].astype(jnp.float32) * scale_factor
    width = gradients_ref.shape[-1]
    for block in (1, 0):
        state, scaling, normed, slope, hidden = stored[block]
        w_up, w_down = weights[block]
        rounded = grad_state.astype(jnp.bfloat16)
        grad_down = contract_rows(hidden, rounded).astype(jnp.bfloat16)
        grad_pre = (against_rows(rounded, w_down[...]) * slope).astype(jnp.bfloat16)
        grad_up = contract_rows(normed, grad_pre).astype(jnp.bfloat16)
        gradients_ref[4 * block] = grad_up[:, :width]
        gradients_ref[4 * block + 1] = grad_up[:, width:]
        gradients_ref[4 * block + 2] = grad_down[:width]
        gradients_ref[4 * block + 3] = grad_down[width:]
        grad_normed = against_rows(grad_pre, w_up[...])
        unit_rows = state * scaling
        grad_state = grad_state + scaling * (
            grad_normed - unit_rows * jnp.mean(grad_normed * unit_rows, axis=-1, keepdims=True)
        )
    grid[...] = grad_state
    number = 0
    for ref, count in zip(returns, back_counts):

        def give(at, carry, ref=ref, number=number):
            first = pl.multiple_of(targets_ref[number + at] * block_rows, block_rows)
            ref[at] = grid[pl.ds(first, block_rows)].astype(jnp.bfloat16)
            return carry

        lax.fori_loop(0, count, give, 0, unroll=count <= 8)
        number += count


def heads(targets, weights, pred_grad, arrived, counts, back_counts, scale_factor):
    rows, channels = pred_grad.shape
    smem = pl.BlockSpec(memory_space=pltpu.SMEM)
    vmem = pl.BlockSpec(memory_space=pltpu.VMEM)
    block_rows = arrived[0].shape[1]
    return pl.pallas_call(
        functools.partial(heads_kernel, counts, back_counts, scale_factor),
        out_shape=(
            jax.ShapeDtypeStruct((rows, channels), jnp.bfloat16),
            jax.ShapeDtypeStruct((8, channels, channels), jnp.bfloat16),
        )
        + tuple(
            jax.ShapeDtypeStruct((count, block_rows, channels), jnp.bfloat16)
            for count in back_counts
        ),
        in_specs=[smem] + [pl.BlockSpec(memory_space=pl.ANY)] * 5 + [vmem] * len(arrived),
        out_specs=(vmem,) * (2 + len(back_counts)),
        scratch_shapes=[
            pltpu.VMEM((rows, channels), jnp.float32),
            *[pltpu.VMEM(weight.shape, weight.dtype) for weight in weights],
            pltpu.VMEM(pred_grad.shape, pred_grad.dtype),
            pltpu.SemaphoreType.DMA((5,)),
        ],
        compiler_params=pltpu.CompilerParams(vmem_limit_bytes=50 * mebibyte),
        name="heads",
    )(targets, *weights, pred_grad, *arrived)


def proj_grad_kernel(
    counts, sources_ref, alive_ref, tiles_ref, encoded_ref, *rest
):
    returned = rest[: len(counts)]
    gradient_ref = rest[len(counts)]
    (rows,) = rest[len(counts) + 1 :]
    block_rows = tiles_ref.shape[1]
    rows[...] = jnp.zeros_like(rows)
    number = 0
    for ref, count in zip(returned, counts):

        def add(at, carry, ref=ref, number=number):
            slot = tile_of(number + at, lax.axis_index("tile"), tiles_ref.shape[0])
            first = pl.multiple_of(sources_ref[slot] * block_rows, block_rows)
            product = contract_rows(tiles_ref[slot], ref[at])
            rows[pl.ds(first, block_rows)] += product * alive_ref[slot].astype(jnp.float32)
            return carry

        lax.fori_loop(0, count, add, 0, unroll=count <= 8)
        number += count
    total = contract_rows(encoded_ref[...], rows[...].astype(jnp.bfloat16))
    gradient_ref[...] = total.astype(jnp.bfloat16).reshape(gradient_ref.shape)


def proj_grad(sources, alive, tiles, encoded, returned, counts):
    tokens, width = encoded.shape
    channels = returned[0].shape[-1]
    smem = pl.BlockSpec(memory_space=pltpu.SMEM)
    vmem = pl.BlockSpec(memory_space=pltpu.VMEM)
    return pl.pallas_call(
        functools.partial(proj_grad_kernel, counts),
        out_shape=jax.ShapeDtypeStruct((8, width // 8, channels), jnp.bfloat16),
        in_specs=[smem] * 2 + [vmem] * (2 + len(returned)),
        out_specs=vmem,
        scratch_shapes=[pltpu.VMEM((tokens, channels), jnp.float32)],
        compiler_params=pltpu.CompilerParams(vmem_limit_bytes=16 * mebibyte),
        name="proj_grad",
    )(sources, alive, tiles, encoded, *returned)


def to_section(array, flip):
    count = lax.axis_size("section")
    return lax.ppermute(array, "section", [(at, at ^ flip) for at in range(count)])


def to_tile(array, flip):
    count = lax.axis_size("tile")
    return lax.ppermute(array, "tile", [(at, at ^ flip) for at in range(count)])


def rows_from(array, first, count):
    return lax.dynamic_slice_in_dim(array, first, count, 0)


def cut_kernel(plan, up_ref, down_ref, *rest):
    outputs, sems = rest[:-1], rest[-1]
    _, _, core, zone = position()
    half = down_ref.shape[0] // 2
    copies = []
    for number, (kind, first, step, count, to) in enumerate(plan[0]):
        start = pl.multiple_of(first + step * zone, 16)
        if kind == "up":
            source = up_ref.at[pl.ds(start, count), pl.ds(pl.multiple_of(core * half, 128), half)]
        else:
            source = down_ref.at[pl.ds(pl.multiple_of(core * half + start, 16), count)]
        output, row = to
        copies.append(
            pltpu.make_async_copy(
                source, outputs[output].at[pl.ds(row, count)], sems.at[number]
            )
        )
    for copy in copies:
        copy.start()
    for copy in copies:
        copy.wait()


def cut(up, down, plan, rows):
    width = down.shape[1]
    hbm = pl.BlockSpec(memory_space=pl.ANY)
    vmem = pl.BlockSpec(memory_space=pltpu.VMEM)
    return pl.pallas_call(
        functools.partial(cut_kernel, (plan,)),
        out_shape=tuple(jax.ShapeDtypeStruct((count, width), up.dtype) for count in rows),
        in_specs=[hbm, hbm],
        out_specs=(vmem,) * len(rows),
        scratch_shapes=[pltpu.SemaphoreType.DMA((len(plan),))],
        compiler_params=pltpu.CompilerParams(vmem_limit_bytes=60 * mebibyte),
        name="cut",
    )(up, down)


def pick_missing(upper, lower, alone):
    zone = position()[3]
    return jnp.concatenate(
        [
            jnp.where(zone == 0, array[:alone], array[array.shape[0] - alone :])
            for array in (upper, lower)
        ]
    )


def gather_layers(own_up, own_down, dst_block):
    half = own_down.shape[0] // 2
    alone = half * 2 // 5 // 16 * 16
    window = half - alone
    x_up, y_down = cut(
        own_up,
        own_down,
        (("up", 0, alone, window, (0, 0)), ("down", 0, alone, window, (1, 0))),
        (window, window),
    )
    table, x_up = lax.optimization_barrier((dst_block, x_up))
    flip = 1
    while flip < lax.axis_size("tile"):
        table = jnp.concatenate([table, to_tile(table, flip)])
        flip *= 2
    table, own_up, own_down = lax.optimization_barrier((table, own_up, own_down))
    down, up = cut(
        own_up, own_down, (("down", 0, 0, half, (0, 0)), ("up", 0, 0, half, (1, 0))), (half, half)
    )
    x_up = to_section(x_up, 1)
    y_down = to_section(y_down, 2)
    x_up, y_down, up, down = lax.optimization_barrier((x_up, y_down, up, down))
    d_down = to_section(y_down, 1)
    d_up = to_section(x_up, 2)
    first_far = to_tile(pick_missing(x_up, y_down, alone), 2)
    other_x_up = to_tile(x_up, 1)
    other_y_down = to_tile(y_down, 1)
    other_x_up, other_y_down, down, up = lax.optimization_barrier(
        (other_x_up, other_y_down, down, up)
    )
    x_down = to_section(down, 1)
    y_up = to_section(up, 2)
    first_far, d_up, d_down = lax.optimization_barrier((first_far, d_up, d_down))
    second_far = to_tile(pick_missing(d_up, d_down, alone), 2)
    parts = {"first_far": first_far, "d_up_window": d_up, "d_down_window": d_down}
    parts.update({"other_" + name: to_tile(part, 1) for name, part in parts.items()})
    last = {"x_down": x_down, "y_up": y_up, "second_far": second_far}
    parts, last = lax.optimization_barrier((parts, last))
    parts.update(last)
    parts.update({"other_" + name: to_tile(part, 1) for name, part in last.items()})
    parts.update({"x_up_window": x_up, "y_down_window": y_down})
    parts.update({"other_x_up_window": other_x_up, "other_y_down_window": other_y_down})
    return parts, table


def add_up(left, *others):
    total = left.astype(jnp.float32)
    for other in others:
        total = total + other.astype(jnp.float32)
    return total.astype(jnp.bfloat16)


def section_share(array, section, core):
    count = lax.axis_size("section")
    mine = rows_from(array, core * count, count)
    others = rows_from(array, (1 - core) * count, count)
    mine = add_up(mine, to_tile(others, 1))

    def pick(number):
        return lax.dynamic_index_in_dim(mine, number, 0, keepdims=False)

    return (pick(section), *[to_section(pick(section ^ flip), flip) for flip in (3, 1, 2)])


def chips_total(share):
    flip = 2
    while flip < lax.axis_size("tile"):
        share = add_up(share, to_tile(share, flip))
        flip *= 2
    return share


def section_shares(share):
    return (share, *[to_section(share, flip) for flip in (1, 2, 3)])


def with_other_core(shares):
    gathered = jnp.stack(shares)
    return (gathered, to_tile(gathered, 1))


def unpack_kernel(gathered_ref, swapped_ref, *outputs):
    section, _, core, _ = position()
    count, rows, columns = gathered_ref.shape
    for side in range(2):
        for number in range(count):
            at = jnp.bitwise_xor(section, number)
            values = jnp.where(
                core == side,
                gathered_ref[at].astype(jnp.float32),
                swapped_ref[at].astype(jnp.float32),
            )
            if len(outputs) == 1:
                outputs[0][pl.ds((side * count + number) * rows, rows)] = values
            elif number < 2:
                outputs[2 * side][:, pl.ds(number * columns, columns)] = values
            else:
                outputs[2 * side + 1][pl.ds((number - 2) * rows, rows)] = values


def unpack(gathered, swapped, shapes):
    vmem = pl.BlockSpec(memory_space=pltpu.VMEM)
    return pl.pallas_call(
        unpack_kernel,
        out_shape=tuple(jax.ShapeDtypeStruct(shape, jnp.float32) for shape in shapes),
        in_specs=[vmem, vmem],
        out_specs=(vmem,) * len(shapes),
        compiler_params=pltpu.CompilerParams(vmem_limit_bytes=16 * mebibyte),
        name="unpack",
    )(gathered, swapped)


def on_device(
    cams,
    vit_up,
    vit_down,
    proj,
    frustum_tiles,
    src_block,
    dst_block,
    live,
    render_up,
    render_down,
    decode_up,
    decode_down,
    pred_grad,
):
    section, _, core, _ = position()
    tile_count = lax.axis_size("tile")
    micro_count = cams.shape[0]
    small = tile_count == 8
    if small:
        pairs = (2, 2, 2, 2)
        singles = (1,) * 8
    else:
        pairs = singles = (tile_count,)

    def cross(sent):
        if not small:
            return [lax.all_to_all(sent[0], "tile", split_axis=0, concat_axis=0, tiled=True)]
        over_near = to_tile(sent[0][1:], 1)
        moved = {flip: to_tile(sent[flip], 2 * flip) for flip in (2, 3)}
        over_near, nearest = lax.optimization_barrier((over_near, sent[1]))
        moved[1] = to_tile(nearest, 2)
        return [sent[0], over_near, *[moved[flip] for flip in (1, 2, 3)]]

    def over(moved):
        if not small:
            return moved
        found = moved[:2]
        for part in moved[2:]:
            found += [part, to_tile(part[1:], 1)]
        return found

    parts, table = gather_layers(vit_up[0], vit_down[0], dst_block)
    encoded, targets, *pieces = encode(
        src_block[0], live[0], table, cams, vit_up[0], vit_down[0], proj,
        frustum_tiles[0], parts, pairs,
    )
    arrived = over(cross(pieces))

    scale_factor = 1.0 / math.sqrt(micro_count * pred_grad.shape[1] * tile_count)
    weights = (render_up, render_down, decode_up, decode_down)
    prediction, gradients, *returns = heads(
        targets, weights, pred_grad[0], arrived, singles, pairs, scale_factor
    )

    moved = cross(returns)
    head_shares = section_share(gradients, section, core)
    *tied, last_share = head_shares
    moved, tied = lax.optimization_barrier((moved, tied))
    head_shares = (*tied, last_share)
    returned = over(moved)
    head_total = chips_total(add_up(*head_shares))
    grad_proj = proj_grad(
        src_block[0], live[0], frustum_tiles[0], encoded, returned, singles
    )
    proj_total = chips_total(add_up(*section_share(grad_proj, section, core)))
    head_shares = with_other_core(section_shares(head_total))
    proj_shares = section_shares(proj_total)
    grads = unpack(
        *head_shares,
        (render_up.shape, render_down.shape, decode_up.shape, decode_down.shape),
    )
    grads, proj_shares = lax.optimization_barrier((grads, with_other_core(proj_shares)))
    (grad_proj,) = unpack(*proj_shares, (proj.shape,))
    return (prediction[None], grad_proj, *grads)


def solution(mesh):
    placed = (
        P(None, "tile", None),
        P("section", None, None),
        P("section", None, None),
        P(),
        P("tile", None, None, None),
        P("tile", None),
        P("tile", None),
        P("tile", None),
        P(),
        P(),
        P(),
        P(),
        P("section", "tile", None),
    )
    return jax.shard_map(
        on_device,
        mesh=mesh,
        in_specs=placed,
        out_specs=(P("section", "tile", None), P(), P(), P(), P(), P()),
        check_vma=False,
    )
```

```python
import functools
import math

import jax
import jax.numpy as jnp
from jax import lax
from jax.experimental import pallas as pl
from jax.experimental.pallas import tpu as pltpu
from jax.sharding import PartitionSpec as P

eps = 1e-05
gelu_inner = math.sqrt(2.0 / math.pi)
gelu_cubic = 0.044715
mebibyte = 1024 * 1024


def gelu(value):
    inner = gelu_inner * (value + gelu_cubic * (value * value * value))
    half = 0.5 * value
    return half + half * jnp.tanh(inner)


def gelu_and_slope(value):
    square = value * value
    reach = jnp.tanh(gelu_inner * value * (1.0 + gelu_cubic * square))
    half = 0.5 * value
    up_to_one = 0.5 + 0.5 * reach
    slope = up_to_one + half * (1.0 - reach * reach) * (
        gelu_inner + (3.0 * gelu_inner * gelu_cubic) * square
    )
    return (value * up_to_one, slope)


def plain(left, right):
    return jnp.dot(left, right, preferred_element_type=jnp.float32)


def contract_rows(left, right):
    return lax.dot_general(
        left, right, (((0,), (0,)), ((), ())), preferred_element_type=jnp.float32
    )


def against_rows(left, right):
    return lax.dot_general(
        left, right, (((1,), (1,)), ((), ())), preferred_element_type=jnp.float32
    )


def position():
    tile = lax.axis_index("tile")
    return (lax.axis_index("section"), tile, tile % 2, tile // 2 % 2)


def tile_of(number, tile, tiles):
    if tiles != 8:
        return number
    chip = jnp.bitwise_xor(number // 2, tile // 2)
    return 2 * chip + jnp.bitwise_xor(number % 2, tile % 2)


def encode_kernel(
    names,
    counts,
    sources_ref,
    alive_ref,
    table_ref,
    cams_ref,
    own_up_ref,
    own_down_ref,
    proj_ref,
    tiles_ref,
    *rest,
):
    parts = dict(zip(names, rest[: len(names)]))
    rest = rest[len(names) :]
    encoded_ref, targets_ref = rest[:2]
    pieces = rest[2 : 2 + len(counts)]
    state, ups, downs, projected, state_sem, up_sems, down_sems = rest[2 + len(counts) :]
    section, tile, core, zone = position()
    layers, halves, half = ups.shape[:3]
    window = parts["x_up_window"].shape[0]
    alone = half - window
    block_rows = tiles_ref.shape[1]

    load_state = pltpu.make_async_copy(cams_ref.at[section], state, state_sem)
    load_state.start()

    def windowed(kind, name, far, number):
        return (
            (kind, name, 0, window, pl.multiple_of(zone * alone, 16)),
            (kind, far, number * alone, alone, pl.multiple_of((1 - zone) * window, 16)),
        )

    where = {
        "x": (*windowed("up", "x_up_window", "first_far", 0), ("down", "x_down", 0, half, 0)),
        "y": (*windowed("down", "y_down_window", "first_far", 1), ("up", "y_up", 0, half, 0)),
        "d": (
            *windowed("up", "d_up_window", "second_far", 0),
            *windowed("down", "d_down_window", "second_far", 1),
        ),
    }
    held = {"up": (ups, up_sems), "down": (downs, down_sems)}

    for layer in range(layers):
        for number, relation in enumerate(("own", "x", "y", "d")):

            @pl.when(jnp.bitwise_xor(section, layer) == number)
            def load(layer=layer, relation=relation):
                if relation == "own":
                    for at in range(halves):
                        pltpu.make_async_copy(
                            own_up_ref.at[:, pl.ds(at * half, half)],
                            ups.at[layer, at],
                            up_sems.at[layer],
                        ).start()
                        pltpu.make_async_copy(
                            own_down_ref.at[pl.ds(at * half, half)],
                            downs.at[layer, at],
                            down_sems.at[layer],
                        ).start()
                    return
                for side, at in (("", core), ("other_", 1 - core)):
                    for kind, name, first, count, to in where[relation]:
                        kept, sems = held[kind]
                        pltpu.make_async_copy(
                            parts[side + name].at[pl.ds(first, count)],
                            kept.at[layer, at, pl.ds(to, count)],
                            sems.at[layer],
                        ).start()

    load_state.wait()
    for layer in range(layers):
        widened = state[...].astype(jnp.float32)
        scaling = lax.rsqrt(jnp.mean(widened * widened, axis=-1, keepdims=True) + eps)
        normed = (widened * scaling).astype(jnp.bfloat16)
        pltpu.make_async_copy(ups.at[layer], ups.at[layer], up_sems.at[layer]).wait()
        pltpu.make_async_copy(downs.at[layer], downs.at[layer], down_sems.at[layer]).wait()
        hidden = [
            gelu(plain(normed, ups[layer, at])).astype(jnp.bfloat16) for at in range(halves)
        ]
        total = widened
        for at in range(halves):
            total = total + plain(hidden[at], downs[layer, at])
        state[...] = total.astype(jnp.bfloat16)
    encoded_ref[...] = state[...]
    projected[...] = plain(state[...], proj_ref[...]).astype(jnp.bfloat16)

    number = 0
    for ref, count in zip(pieces, counts):

        def slot(at, carry, ref=ref, number=number):
            tile_at = tile_of(number + at, tile, tiles_ref.shape[0])
            first = pl.multiple_of(sources_ref[tile_at] * block_rows, block_rows)
            piece = plain(tiles_ref[tile_at], projected[pl.ds(first, block_rows)])
            piece = piece * alive_ref[tile_at].astype(jnp.float32)
            ref[at] = piece.astype(jnp.bfloat16)
            targets_ref[number + at] = table_ref[jnp.bitwise_xor(tile_at, tile), tile]
            return carry

        lax.fori_loop(0, count, slot, 0, unroll=count <= 8)
        number += count


def encode(
    sources, alive, table, cams, own_up, own_down, proj, tiles, parts, counts
):
    names = tuple(parts)
    tokens, width = cams.shape[1:]
    hidden = own_up.shape[1]
    layers = cams.shape[0]
    half = hidden // 2
    block_rows = tiles.shape[1]
    channels = proj.shape[1]
    smem = pl.BlockSpec(memory_space=pltpu.SMEM)
    vmem = pl.BlockSpec(memory_space=pltpu.VMEM)
    hbm = pl.BlockSpec(memory_space=pl.ANY)
    return pl.pallas_call(
        functools.partial(encode_kernel, names, counts),
        out_shape=(
            jax.ShapeDtypeStruct((tokens, width), jnp.bfloat16),
            jax.ShapeDtypeStruct(sources.shape, jnp.int32),
        )
        + tuple(
            jax.ShapeDtypeStruct((count, block_rows, channels), jnp.bfloat16) for count in counts
        ),
        in_specs=[smem] * 3 + [hbm] * 3 + [vmem] * 2 + [hbm] * len(names),
        out_specs=(vmem, smem) + (vmem,) * len(counts),
        scratch_shapes=[
            pltpu.VMEM((tokens, width), jnp.bfloat16),
            pltpu.VMEM((layers, 2, width, half), jnp.bfloat16),
            pltpu.VMEM((layers, 2, half, width), jnp.bfloat16),
            pltpu.VMEM((tokens, channels), jnp.bfloat16),
            pltpu.SemaphoreType.DMA,
            pltpu.SemaphoreType.DMA((layers,)),
            pltpu.SemaphoreType.DMA((layers,)),
        ],
        compiler_params=pltpu.CompilerParams(vmem_limit_bytes=50 * mebibyte),
        name="encode",
    )(sources, alive, table, cams, own_up, own_down, proj, tiles, *parts.values())


def heads_kernel(
    counts,
    back_counts,
    scale_factor,
    targets_ref,
    render_up_ref,
    render_down_ref,
    decode_up_ref,
    decode_down_ref,
    pred_grad_ref,
    *rest,
):
    arrived = rest[: len(counts)]
    prediction_ref, gradients_ref = rest[len(counts) : len(counts) + 2]
    returns = rest[len(counts) + 2 : -7]
    grid = rest[-7]
    sems = rest[-1]
    loads = [
        pltpu.make_async_copy(source, held, sems.at[at])
        for at, (source, held) in enumerate(
            zip(
                (render_up_ref, render_down_ref, decode_up_ref, decode_down_ref, pred_grad_ref),
                rest[-6:-1],
            )
        )
    ]
    for load in loads:
        load.start()
    render_up_ref, render_down_ref, decode_up_ref, decode_down_ref, pred_grad_ref = rest[-6:-1]
    block_rows = arrived[0].shape[1]
    rows = grid.shape[0]

    grid[...] = jnp.zeros_like(grid)
    number = 0
    for ref, count in zip(arrived, counts):

        def add(at, carry, ref=ref, number=number):
            first = pl.multiple_of(targets_ref[number + at] * block_rows, block_rows)
            grid[pl.ds(first, block_rows)] += ref[at].astype(jnp.float32)
            return carry

        lax.fori_loop(0, count, add, 0, unroll=count <= 8)
        number += count

    for load in loads:
        load.wait()
    weights = ((render_up_ref, render_down_ref), (decode_up_ref, decode_down_ref))
    state = grid[...]
    stored = []
    for w_up, w_down in weights:
        scaling = lax.rsqrt(jnp.mean(state * state, axis=-1, keepdims=True) + eps)
        normed = (state * scaling).astype(jnp.bfloat16)
        value, slope = gelu_and_slope(plain(normed, w_up[...]))
        hidden = value.astype(jnp.bfloat16)
        stored.append((state, scaling, normed, slope, hidden))
        state = state + plain(hidden, w_down[...])
    prediction_ref[...] = state.astype(jnp.bfloat16)

    grad_state = pred_grad_ref[...].astype(jnp.float32) * scale_factor
    width = gradients_ref.shape[-1]
    for block in (1, 0):
        state, scaling, normed, slope, hidden = stored[block]
        w_up, w_down = weights[block]
        rounded = grad_state.astype(jnp.bfloat16)
        grad_down = contract_rows(hidden, rounded).astype(jnp.bfloat16)
        grad_pre = (against_rows(rounded, w_down[...]) * slope).astype(jnp.bfloat16)
        grad_up = contract_rows(normed, grad_pre).astype(jnp.bfloat16)
        gradients_ref[4 * block] = grad_up[:, :width]
        gradients_ref[4 * block + 1] = grad_up[:, width:]
        gradients_ref[4 * block + 2] = grad_down[:width]
        gradients_ref[4 * block + 3] = grad_down[width:]
        grad_normed = against_rows(grad_pre, w_up[...])
        unit_rows = state * scaling
        grad_state = grad_state + scaling * (
            grad_normed - unit_rows * jnp.mean(grad_normed * unit_rows, axis=-1, keepdims=True)
        )
    grid[...] = grad_state
    number = 0
    for ref, count in zip(returns, back_counts):

        def give(at, carry, ref=ref, number=number):
            first = pl.multiple_of(targets_ref[number + at] * block_rows, block_rows)
            ref[at] = grid[pl.ds(first, block_rows)].astype(jnp.bfloat16)
            return carry

        lax.fori_loop(0, count, give, 0, unroll=count <= 8)
        number += count


def heads(targets, weights, pred_grad, arrived, counts, back_counts, scale_factor):
    rows, channels = pred_grad.shape
    smem = pl.BlockSpec(memory_space=pltpu.SMEM)
    vmem = pl.BlockSpec(memory_space=pltpu.VMEM)
    block_rows = arrived[0].shape[1]
    return pl.pallas_call(
        functools.partial(heads_kernel, counts, back_counts, scale_factor),
        out_shape=(
            jax.ShapeDtypeStruct((rows, channels), jnp.bfloat16),
            jax.ShapeDtypeStruct((8, channels, channels), jnp.bfloat16),
        )
        + tuple(
            jax.ShapeDtypeStruct((count, block_rows, channels), jnp.bfloat16)
            for count in back_counts
        ),
        in_specs=[smem] + [pl.BlockSpec(memory_space=pl.ANY)] * 5 + [vmem] * len(arrived),
        out_specs=(vmem,) * (2 + len(back_counts)),
        scratch_shapes=[
            pltpu.VMEM((rows, channels), jnp.float32),
            *[pltpu.VMEM(weight.shape, weight.dtype) for weight in weights],
            pltpu.VMEM(pred_grad.shape, pred_grad.dtype),
            pltpu.SemaphoreType.DMA((5,)),
        ],
        compiler_params=pltpu.CompilerParams(vmem_limit_bytes=50 * mebibyte),
        name="heads",
    )(targets, *weights, pred_grad, *arrived)


def proj_grad_kernel(
    counts, sources_ref, alive_ref, tiles_ref, encoded_ref, *rest
):
    returned = rest[: len(counts)]
    gradient_ref = rest[len(counts)]
    (rows,) = rest[len(counts) + 1 :]
    block_rows = tiles_ref.shape[1]
    rows[...] = jnp.zeros_like(rows)
    number = 0
    for ref, count in zip(returned, counts):

        def add(at, carry, ref=ref, number=number):
            slot = tile_of(number + at, lax.axis_index("tile"), tiles_ref.shape[0])
            first = pl.multiple_of(sources_ref[slot] * block_rows, block_rows)
            product = contract_rows(tiles_ref[slot], ref[at])
            rows[pl.ds(first, block_rows)] += product * alive_ref[slot].astype(jnp.float32)
            return carry

        lax.fori_loop(0, count, add, 0, unroll=count <= 8)
        number += count
    total = contract_rows(encoded_ref[...], rows[...].astype(jnp.bfloat16))
    gradient_ref[...] = total.astype(jnp.bfloat16).reshape(gradient_ref.shape)


def proj_grad(sources, alive, tiles, encoded, returned, counts):
    tokens, width = encoded.shape
    channels = returned[0].shape[-1]
    smem = pl.BlockSpec(memory_space=pltpu.SMEM)
    vmem = pl.BlockSpec(memory_space=pltpu.VMEM)
    return pl.pallas_call(
        functools.partial(proj_grad_kernel, counts),
        out_shape=jax.ShapeDtypeStruct((8, width // 8, channels), jnp.bfloat16),
        in_specs=[smem] * 2 + [vmem] * (2 + len(returned)),
        out_specs=vmem,
        scratch_shapes=[pltpu.VMEM((tokens, channels), jnp.float32)],
        compiler_params=pltpu.CompilerParams(vmem_limit_bytes=16 * mebibyte),
        name="proj_grad",
    )(sources, alive, tiles, encoded, *returned)


def to_section(array, flip):
    count = lax.axis_size("section")
    return lax.ppermute(array, "section", [(at, at ^ flip) for at in range(count)])


def to_tile(array, flip):
    count = lax.axis_size("tile")
    return lax.ppermute(array, "tile", [(at, at ^ flip) for at in range(count)])


def rows_from(array, first, count):
    return lax.dynamic_slice_in_dim(array, first, count, 0)


def cut_kernel(plan, up_ref, down_ref, *rest):
    outputs, sems = rest[:-1], rest[-1]
    _, _, core, zone = position()
    half = down_ref.shape[0] // 2
    copies = []
    for number, (kind, first, step, count, to) in enumerate(plan[0]):
        start = pl.multiple_of(first + step * zone, 16)
        if kind == "up":
            source = up_ref.at[pl.ds(start, count), pl.ds(pl.multiple_of(core * half, 128), half)]
        else:
            source = down_ref.at[pl.ds(pl.multiple_of(core * half + start, 16), count)]
        output, row = to
        copies.append(
            pltpu.make_async_copy(
                source, outputs[output].at[pl.ds(row, count)], sems.at[number]
            )
        )
    for copy in copies:
        copy.start()
    for copy in copies:
        copy.wait()


def cut(up, down, plan, rows):
    width = down.shape[1]
    hbm = pl.BlockSpec(memory_space=pl.ANY)
    vmem = pl.BlockSpec(memory_space=pltpu.VMEM)
    return pl.pallas_call(
        functools.partial(cut_kernel, (plan,)),
        out_shape=tuple(jax.ShapeDtypeStruct((count, width), up.dtype) for count in rows),
        in_specs=[hbm, hbm],
        out_specs=(vmem,) * len(rows),
        scratch_shapes=[pltpu.SemaphoreType.DMA((len(plan),))],
        compiler_params=pltpu.CompilerParams(vmem_limit_bytes=60 * mebibyte),
        name="cut",
    )(up, down)


def pick_missing(upper, lower, alone):
    zone = position()[3]
    return jnp.concatenate(
        [
            jnp.where(zone == 0, array[:alone], array[array.shape[0] - alone :])
            for array in (upper, lower)
        ]
    )


def gather_layers(own_up, own_down, dst_block):
    half = own_down.shape[0] // 2
    alone = half * 2 // 5 // 16 * 16
    window = half - alone
    x_up, y_down = cut(
        own_up,
        own_down,
        (("up", 0, alone, window, (0, 0)), ("down", 0, alone, window, (1, 0))),
        (window, window),
    )
    table, x_up = lax.optimization_barrier((dst_block, x_up))
    flip = 1
    while flip < lax.axis_size("tile"):
        table = jnp.concatenate([table, to_tile(table, flip)])
        flip *= 2
    table, own_up, own_down = lax.optimization_barrier((table, own_up, own_down))
    down, up = cut(
        own_up, own_down, (("down", 0, 0, half, (0, 0)), ("up", 0, 0, half, (1, 0))), (half, half)
    )
    x_up = to_section(x_up, 1)
    y_down = to_section(y_down, 2)
    x_up, y_down, up, down = lax.optimization_barrier((x_up, y_down, up, down))
    d_down = to_section(y_down, 1)
    d_up = to_section(x_up, 2)
    first_far = to_tile(pick_missing(x_up, y_down, alone), 2)
    other_x_up = to_tile(x_up, 1)
    other_y_down = to_tile(y_down, 1)
    other_x_up, other_y_down, down, up = lax.optimization_barrier(
        (other_x_up, other_y_down, down, up)
    )
    x_down = to_section(down, 1)
    y_up = to_section(up, 2)
    first_far, d_up, d_down = lax.optimization_barrier((first_far, d_up, d_down))
    second_far = to_tile(pick_missing(d_up, d_down, alone), 2)
    parts = {"first_far": first_far, "d_up_window": d_up, "d_down_window": d_down}
    parts.update({"other_" + name: to_tile(part, 1) for name, part in parts.items()})
    last = {"x_down": x_down, "y_up": y_up, "second_far": second_far}
    parts, last = lax.optimization_barrier((parts, last))
    parts.update(last)
    parts.update({"other_" + name: to_tile(part, 1) for name, part in last.items()})
    parts.update({"x_up_window": x_up, "y_down_window": y_down})
    parts.update({"other_x_up_window": other_x_up, "other_y_down_window": other_y_down})
    return parts, table


def add_up(left, *others):
    total = left.astype(jnp.float32)
    for other in others:
        total = total + other.astype(jnp.float32)
    return total.astype(jnp.bfloat16)


def section_share(array, section, core):
    count = lax.axis_size("section")
    mine = rows_from(array, core * count, count)
    others = rows_from(array, (1 - core) * count, count)
    mine = add_up(mine, to_tile(others, 1))

    def pick(number):
        return lax.dynamic_index_in_dim(mine, number, 0, keepdims=False)

    return (pick(section), *[to_section(pick(section ^ flip), flip) for flip in (3, 1, 2)])


def chips_total(share):
    flip = 2
    while flip < lax.axis_size("tile"):
        share = add_up(share, to_tile(share, flip))
        flip *= 2
    return share


def section_shares(share):
    return (share, *[to_section(share, flip) for flip in (1, 2, 3)])


def section_shares_doubled(share):
    across = jnp.stack([share, to_section(share, 2)])
    beside = to_section(across, 1)
    return (across[0], beside[0], across[1], beside[1])


def with_other_core(shares):
    gathered = jnp.stack(shares)
    return (gathered, to_tile(gathered, 1))


def unpack_kernel(gathered_ref, swapped_ref, *outputs):
    section, _, core, _ = position()
    count, rows, columns = gathered_ref.shape
    for side in range(2):
        for number in range(count):
            at = jnp.bitwise_xor(section, number)
            values = jnp.where(
                core == side,
                gathered_ref[at].astype(jnp.float32),
                swapped_ref[at].astype(jnp.float32),
            )
            if len(outputs) == 1:
                outputs[0][pl.ds((side * count + number) * rows, rows)] = values
            elif number < 2:
                outputs[2 * side][:, pl.ds(number * columns, columns)] = values
            else:
                outputs[2 * side + 1][pl.ds((number - 2) * rows, rows)] = values


def unpack(gathered, swapped, shapes):
    vmem = pl.BlockSpec(memory_space=pltpu.VMEM)
    return pl.pallas_call(
        unpack_kernel,
        out_shape=tuple(jax.ShapeDtypeStruct(shape, jnp.float32) for shape in shapes),
        in_specs=[vmem, vmem],
        out_specs=(vmem,) * len(shapes),
        compiler_params=pltpu.CompilerParams(vmem_limit_bytes=16 * mebibyte),
        name="unpack",
    )(gathered, swapped)


def on_device(
    cams,
    vit_up,
    vit_down,
    proj,
    frustum_tiles,
    src_block,
    dst_block,
    live,
    render_up,
    render_down,
    decode_up,
    decode_down,
    pred_grad,
):
    section, _, core, _ = position()
    tile_count = lax.axis_size("tile")
    micro_count = cams.shape[0]
    small = tile_count == 8
    if small:
        pairs = (2, 2, 2, 2)
        singles = (1,) * 8
    else:
        pairs = singles = (tile_count,)

    def cross(sent):
        if not small:
            return [lax.all_to_all(sent[0], "tile", split_axis=0, concat_axis=0, tiled=True)]
        over_near = to_tile(sent[0][1:], 1)
        moved = {flip: to_tile(sent[flip], 2 * flip) for flip in (2, 3)}
        over_near, nearest = lax.optimization_barrier((over_near, sent[1]))
        moved[1] = to_tile(nearest, 2)
        return [sent[0], over_near, *[moved[flip] for flip in (1, 2, 3)]]

    def over(moved):
        if not small:
            return moved
        found = moved[:2]
        for part in moved[2:]:
            found += [part, to_tile(part[1:], 1)]
        return found

    parts, table = gather_layers(vit_up[0], vit_down[0], dst_block)
    encoded, targets, *pieces = encode(
        src_block[0], live[0], table, cams, vit_up[0], vit_down[0], proj,
        frustum_tiles[0], parts, pairs,
    )
    arrived = over(cross(pieces))

    scale_factor = 1.0 / math.sqrt(micro_count * pred_grad.shape[1] * tile_count)
    weights = (render_up, render_down, decode_up, decode_down)
    prediction, gradients, *returns = heads(
        targets, weights, pred_grad[0], arrived, singles, pairs, scale_factor
    )

    moved = cross(returns)
    head_shares = section_share(gradients, section, core)
    *tied, last_share = head_shares
    moved, tied = lax.optimization_barrier((moved, tied))
    head_shares = (*tied, last_share)
    returned = over(moved)
    head_total = chips_total(add_up(*head_shares))
    grad_proj = proj_grad(
        src_block[0], live[0], frustum_tiles[0], encoded, returned, singles
    )
    proj_total = chips_total(add_up(*section_share(grad_proj, section, core)))
    head_shares = with_other_core(section_shares_doubled(head_total))
    proj_shares = section_shares(proj_total)
    grads = unpack(
        *head_shares,
        (render_up.shape, render_down.shape, decode_up.shape, decode_down.shape),
    )
    grads, proj_shares = lax.optimization_barrier((grads, with_other_core(proj_shares)))
    (grad_proj,) = unpack(*proj_shares, (proj.shape,))
    return (prediction[None], grad_proj, *grads)


def solution(mesh):
    placed = (
        P(None, "tile", None),
        P("section", None, None),
        P("section", None, None),
        P(),
        P("tile", None, None, None),
        P("tile", None),
        P("tile", None),
        P("tile", None),
        P(),
        P(),
        P(),
        P(),
        P("section", "tile", None),
    )
    return jax.shard_map(
        on_device,
        mesh=mesh,
        in_specs=placed,
        out_specs=(P("section", "tile", None), P(), P(), P(), P(), P()),
        check_vma=False,
    )
```
